128 devices in a mesh: ctx: 16 (over x_hi, z, core), tp: 8 (over y, x_lo).
Axes of the slice: x: 4 (x_hi: 2, x_lo: 2; x = x_hi * 2 + x_lo), y: 4, z: 4, core: 2. Of those that a mesh axis runs over, the one named last changes fastest.
Arguments:
- features: bfloat16 [16384, 3, 8192], P('ctx', None, 'tp'), may hold values from -6 to 6
- contig_starts: int32 [128], P('ctx'), may hold values 0 or 1
- short_filter: float32 [7, 3, 8192], P(None, None, 'tp'), may hold values from -2.4 to 2.4
- medium_filter: float32 [512, 128], P('tp'), may hold values from -0.54 to 0.54
- filter_bias: float32 [8192], P('tp'), may hold values from -4 to 4
- out_weight: bfloat16 [8192, 8192], P('tp', 'ctx'), may hold values from -0.0625 to 0.0625
Outputs:
- mixed: bfloat16 [16384, 8192], P('ctx', 'tp')
The draws below stay inside these ranges and needn't reach their ends.
All inputs are finite; a program needn't handle non-finite values. No bound on the sum of `contig_starts` on one device may be relied on, other than what follows from the above.
Results may differ from the reference program's by a relative error of at most 0.017.
Values may be sent and summed in bfloat16 or wider, within the bound.
A program may use at most 128 MiB of HBM per device.

```python
import jax
import jax.numpy as jnp
from jax import lax

D = 8192
BLOCK = 128
SHORT = 7
GROUP_CH = 16
TOKENS = 16384
NBLOCKS = 128
GROUPS = 512
N_TP = 8


def touch_ends(drawn, own_key, least, top_value):
    spot = [jax.random.randint(jax.random.fold_in(own_key, axis), (), 0, length) for axis, length in enumerate(drawn.shape)]
    main_axis = drawn.shape.index(max(drawn.shape))
    next_to = spot[:main_axis] + [(spot[main_axis] + 1) % drawn.shape[main_axis]] + spot[main_axis + 1:]
    return drawn.at[tuple(spot)].set(least).at[tuple(next_to)].set(top_value)


def steps_of(stream_key, dims, cuts, least, largest):
    def one(dim, parts):
        steps = jax.random.uniform(jax.random.fold_in(jax.random.fold_in(stream_key, 6), dim), (parts,), jnp.float32, least / len(cuts), largest / len(cuts))
        return jnp.repeat(jnp.exp(steps), dims[dim] // parts).reshape((-1,) + (1,) * (len(dims) - dim - 1))

    level = one(*cuts[0])
    for cut in cuts[1:]:
        level = level * one(*cut)
    return level


def noise(own_key, extent, scale, reach, cuts=(), kind=jnp.bfloat16):
    drawn = scale * jax.random.normal(own_key, extent, jnp.float32)
    if cuts:
        drawn = drawn * steps_of(own_key, extent, cuts, -0.22, 0.18)
    return jnp.clip(drawn, -reach, reach).astype(kind)


def setup_inputs(seed: int = 0) -> dict:
    splits = jax.random.split(jax.random.key(seed), 7)
    return {
        "features": noise(splits[0], (TOKENS, 3, D), 1.0, 6.0, ((0, 16), (2, 8))),
        "contig_starts": touch_ends((jax.random.randint(splits[1], (NBLOCKS,), 0, 4) < 1).astype(jnp.int32), jax.random.fold_in(splits[1], 1), 0, 1),
        "short_filter": noise(splits[2], (SHORT, 3, D), 0.4, 2.4, ((2, 8),), jnp.float32),
        "medium_filter": noise(splits[3], (GROUPS, BLOCK), 0.09, 0.54, ((0, 8),), jnp.float32),
        "filter_bias": noise(splits[4], (D,), 1.0, 4.0, ((0, 8),), jnp.float32),
        "out_weight": noise(splits[5], (D, D), D ** -0.5, 0.0625, ((0, 8), (1, 16))),
    }


def short_conv(ext, weights, block):
    span = weights.shape[0]
    total = weights[0] * ext[:, span - 1:span - 1 + block]
    for lag in range(1, span):
        total = total + weights[lag] * ext[:, span - 1 - lag:span - 1 - lag + block]
    return total


def toeplitz(taps):
    width = taps.shape[1]
    rows = jnp.arange(width)[:, None]
    cols = jnp.arange(width)[None, :]
    lag = rows - cols
    zero = jnp.zeros((), taps.dtype)
    near = jnp.where(lag >= 0, taps[:, jnp.clip(lag, 0, width - 1)], zero)
    far = jnp.where(lag < 0, taps[:, jnp.clip(lag + width, 0, width - 1)], zero)
    return near, far


def reference(features, contig_starts, short_filter, medium_filter, filter_bias, out_weight):
    nblk = TOKENS // BLOCK
    keep = (1 - contig_starts).astype(jnp.float32)
    blocks = features.astype(jnp.float32).reshape(nblk, BLOCK, 3, D)
    tails = blocks[:, BLOCK - (SHORT - 1):]
    before = jnp.concatenate([jnp.zeros((1, SHORT - 1, 3, D), jnp.float32), tails[:-1]], axis=0)
    before = before * keep[:, None, None, None]
    ext = jnp.concatenate([before, blocks], axis=1)
    filtered = short_conv(ext, short_filter, BLOCK)
    gated = (filtered[:, :, 1] * filtered[:, :, 2]).astype(jnp.bfloat16)
    near, far = toeplitz(medium_filter.astype(jnp.bfloat16))
    groups = D // GROUP_CH
    grouped = gated.reshape(nblk, BLOCK, groups, GROUP_CH)
    earlier = jnp.concatenate([jnp.zeros((1, BLOCK, groups, GROUP_CH), jnp.float32), grouped[:-1].astype(jnp.float32)], axis=0)
    earlier = earlier * keep[:, None, None, None]
    conv = jnp.einsum("gij,bjgc->bigc", near.astype(jnp.float32), grouped.astype(jnp.float32))
    conv = conv + jnp.einsum("gij,bjgc->bigc", far.astype(jnp.float32), earlier)
    conv = conv.reshape(nblk, BLOCK, D)
    mixer = (filtered[:, :, 0] * (conv + filter_bias * gated.astype(jnp.float32))).astype(jnp.bfloat16)
    mixer = mixer.reshape(TOKENS, D)
    width = D // N_TP

    def add_group(total, index):
        start = (index * width).astype(jnp.int32)
        cols = lax.dynamic_slice_in_dim(mixer, start, width, 1)
        rows = lax.dynamic_slice_in_dim(out_weight, start, width, 0)
        part = jnp.dot(cols, rows, preferred_element_type=jnp.float32).astype(jnp.bfloat16)
        return total + part.astype(jnp.float32), None

    total, _ = lax.scan(add_group, jnp.zeros((TOKENS, D), jnp.float32), jnp.arange(N_TP, dtype=jnp.int32))
    return total.astype(jnp.bfloat16)
```

```python
import jax
import jax.numpy as jnp
from jax import lax
from jax.experimental import pallas as pl
from jax.experimental.pallas import tpu as pltpu
from jax.sharding import PartitionSpec as P

MESH = pl.DeviceIdType.MESH
F32 = jnp.float32
BF16 = jnp.bfloat16

ROWS = 1024
CH = 1024
BLK = 128
NB = ROWS // BLK
SPAN = 7
HALO = 16
GROUP = 16
LANES = 128
PER_TILE = LANES // GROUP
CHUNK = 256
NCHUNK = ROWS // CHUNK


def unit_of(kind, u):
    late, v = u // 4, u % 4
    plain = 2 * (v % 2) + v // 2
    swapped = 2 * (1 - v % 2) + v // 2
    dy0, h0 = 2 - 2 * late, plain
    dy1, h1 = 1 + 2 * (v % 2), late * plain + (1 - late) * swapped
    return dy0 + kind * (dy1 - dy0), h0 + kind * (h1 - h0)


def kernel(
    feats, starts, sw, rtaps, bias, w_ref, out_ref,
    fbuf, ext, gbuf, toep, xs, conv, mix, wts, part, got1, got2,
    f_sem, halo_ss, halo_rs, w_rs, sib_ss, zp_ss, zm_ss, x_ss, mix_ss, mix_rs,
    p_ss, got1_rs, got2_rs,
):
    c, t = lax.axis_index("ctx"), lax.axis_index("tp")
    xh, z, k = c // 8, (c // 2) % 4, c % 2
    y, xl = t // 2, t % 2
    role = (xl + z) % 2

    def dev(xh, z, k, y, xl):
        return ((xh * 4 + z) * 2 + k, y * 2 + xl)

    sib = dev(xh, z, 1 - k, y, xl)
    zp, zm = dev(xh, (z + 1) % 4, k, y, xl), dev(xh, (z + 3) % 4, k, y, xl)
    yp, ym = dev(xh, z, k, (y + 1) % 4, xl), dev(xh, z, k, (y + 3) % 4, xl)
    xp, xn, x2 = dev(xh, z, k, y, 1 - xl), dev(1 - xh, z, k, y, 1 - xl), dev(1 - xh, z, k, y, xl)
    nxt, prv = ((c + 1) % 16, t), ((c + 15) % 16, t)

    f_copies = []
    for s in range(3):
        cp = pltpu.make_async_copy(feats.at[s], fbuf.at[s, pl.ds(HALO, ROWS)], f_sem.at[s])
        cp.start()
        f_copies.append(cp)

    barrier = pltpu.get_barrier_semaphore()
    for d in (sib, zp, zm, yp, ym, xp, xn, x2, prv):
        pl.semaphore_signal(barrier, inc=1, device_id=d, device_id_type=MESH)
    pl.semaphore_wait(barrier, 9)

    def remote(src, dst, ss, rs, d):
        return pltpu.make_async_remote_copy(
            src_ref=src, dst_ref=dst, send_sem=ss, recv_sem=rs, device_id=d, device_id_type=MESH
        )

    dy_own = (2 * xh + z // 2 - y + 4) % 4

    def w_piece(h):
        return w_ref.at[:, pl.ds(h * LANES, LANES)]

    def slot(dy, h, r, core):
        return wts.at[dy, h, r, :, pl.ds(pl.multiple_of(core * LANES, LANES), LANES)]

    def x_copy(h, r, d, i):
        return remote(w_piece(h), slot(dy_own, h, r, k), x_ss.at[h, i], w_rs.at[dy_own, h, r, k], d)

    halo_f = remote(
        feats.at[:, pl.ds(ROWS - HALO, HALO)], fbuf.at[:, pl.ds(0, HALO)], halo_ss.at[0], halo_rs.at[0], nxt
    )
    halo_f.start()

    @pl.when(role == 0)
    def _():
        for h in (0, 2, 1, 3):
            pltpu.make_async_copy(w_piece(h), slot(dy_own, h, 0, k), w_rs.at[dy_own, h, 0, k]).start()
            x_copy(h, 0, x2, 0).start()

    @pl.when(role == 1)
    def _():
        for h in (0, 2, 1, 3):
            x_copy(h, 1, xp, 0).start()
            x_copy(h, 1, xn, 1).start()

    def sib_copy(dy, h, r):
        here = slot(dy, h, r, k)
        return remote(here, here, sib_ss.at[dy, h, r], w_rs.at[dy, h, r, k], sib)

    def zp_copy(dy, h, r):
        here = slot(dy, h, r, k)
        return remote(here, here, zp_ss.at[dy, h, r], w_rs.at[dy, h, r, k], zp)

    def zm_copy(dy, h, r):
        here = slot(dy, h, r, k)
        return remote(here, here, zm_ss.at[dy, h, r], w_rs.at[dy, h, r, k], zm)

    def w_wait(dy, h, r, core):
        here = slot(dy, h, r, core)
        remote(here, here, sib_ss.at[dy, h, r], w_rs.at[dy, h, r, core], sib).wait_recv()

    kind_here = (z // 2 + y) % 2
    kind_below = (((z + 3) % 4) // 2 + y) % 2

    def spread(lo, hi):
        @pl.when(role == 0)
        def _():
            def body(u, _):
                dy, h = unit_of(kind_here, u)
                for r in range(2):
                    w_wait(dy, h, r, k)
                    zp_copy(dy, h, r).start()
                    zm_copy(dy, h, r).start()
                    sib_copy(dy, h, r).start()
                return 0

            lax.fori_loop(lo, hi, body, 0)

    def relay(lo, hi):
        @pl.when(role == 0)
        def _():
            def body(u, _):
                dy, h = unit_of(1 - kind_here, u)
                for r in range(2):
                    w_wait(dy, h, r, k)
                    sib_copy(dy, h, r).start()
                return 0

            lax.fori_loop(lo, hi, body, 0)

        @pl.when(role == 1)
        def _():
            def body(u, _):
                dya, ha = unit_of(kind_below, u)
                dyb, hb = unit_of(1 - kind_below, u)
                for r in range(2):
                    w_wait(dya, ha, r, k)
                    if r == 0:
                        zp_copy(dya, ha, r).start()
                    sib_copy(dya, ha, r).start()
                    w_wait(dyb, hb, r, k)
                    if r == 1:
                        zm_copy(dyb, hb, r).start()
                    sib_copy(dyb, hb, r).start()
                return 0

            lax.fori_loop(lo, hi, body, 0)

    def toep_body(g, _):
        row = jnp.broadcast_to(rtaps[pl.ds(g, 1)], (BLK, 2 * BLK))
        toep[g] = pltpu.roll(row, 1, 1, stride=1, stride_axis=0).astype(BF16)
        return 0

    lax.fori_loop(0, CH // GROUP, toep_body, 0)

    first = (c > 0).astype(F32)

    def keep_of(b):
        kept = (1 - starts[b]).astype(F32)
        return kept * jnp.where(b == 0, first, 1.0)

    def short(s, b, keep, lanes):
        tail = fbuf[s, pl.ds(pl.multiple_of(b * BLK, BLK), HALO), lanes].astype(F32)
        ext[s, pl.ds(0, 8), lanes] = tail[8:] * keep
        ext[s, pl.ds(8, BLK), lanes] = fbuf[
            s, pl.ds(pl.multiple_of(b * BLK + HALO, HALO), BLK), lanes
        ].astype(F32)
        total = sw[s, pl.ds(0, 1), lanes] * ext[s, pl.ds(8, BLK), lanes]
        for j in range(1, SPAN):
            total += sw[s, pl.ds(j, 1), lanes] * ext[s, pl.ds(8 - j, BLK), lanes]
        return total

    def lanes_of(lt):
        return pl.ds(pl.multiple_of(lt * LANES, LANES), LANES)

    def gate(b):
        keep = keep_of(b)

        def body(lt, _):
            lanes = lanes_of(lt)
            gbuf[b + 1, :, lanes] = (short(1, b, keep, lanes) * short(2, b, keep, lanes)).astype(BF16)
            return 0

        lax.fori_loop(0, CH // LANES, body, 0)

    for cp in f_copies:
        cp.wait()
    gate(NB - 1)
    halo_g = remote(gbuf.at[NB], gbuf.at[0], halo_ss.at[1], halo_rs.at[1], nxt)
    halo_g.start()

    def gate_body(i, _):
        gate(NB - 2 - i)
        return 0

    lax.fori_loop(0, NB - 2, gate_body, 0)
    halo_f.wait_recv()
    gate(0)
    spread(0, 4)

    def mix_copy(m):
        rows = pl.ds(m * CHUNK, CHUNK)
        return remote(mix.at[0, rows], mix.at[1, rows], mix_ss.at[m], mix_rs.at[m], xp)

    lane_group = lax.broadcasted_iota(jnp.int32, (BLK, 2 * LANES), 1) % LANES // GROUP

    def mix_pair(b0):
        keeps = [keep_of(b0), keep_of(b0 + 1)]

        def body(lt, _):
            lanes = lanes_of(lt)
            for i in range(2):
                cols = pl.ds(i * LANES, LANES)
                xs[pl.ds(0, BLK), cols] = (gbuf[b0 + i, :, lanes].astype(F32) * keeps[i]).astype(BF16)
                xs[pl.ds(BLK, BLK), cols] = gbuf[b0 + i + 1, :, lanes]
            mats = toep[pl.ds(lt * PER_TILE, PER_TILE)].reshape(PER_TILE * BLK, 2 * BLK)
            every = jnp.dot(mats, xs[...], preferred_element_type=F32)
            every = every.reshape(PER_TILE, BLK, 2 * LANES)
            picked = every[0]
            for g in range(1, PER_TILE):
                picked = jnp.where(lane_group == g, every[g], picked)
            conv[...] = picked
            for i in range(2):
                gated = gbuf[b0 + i + 1, :, lanes].astype(F32)
                query = short(0, b0 + i, keeps[i], lanes)
                direct = conv[:, pl.ds(i * LANES, LANES)] + bias[:, lanes] * gated
                mix[0, pl.ds(pl.multiple_of((b0 + i) * BLK, BLK), BLK), lanes] = (query * direct).astype(BF16)
            return 0

        lax.fori_loop(0, CH // LANES, body, 0)

    chunk_at = [NCHUNK - 1 - i for i in range(NCHUNK)]

    def chunk_body(i, _):
        m = NCHUNK - 1 - i
        mix_pair(2 * m)
        mix_copy(m).start()
        return 0

    lax.fori_loop(0, NCHUNK - 1, chunk_body, 0)
    spread(4, 8)
    halo_g.wait_recv()
    chunk_body(NCHUNK - 1, 0)

    def rows_of(m):
        return pl.ds(pl.multiple_of(m * CHUNK, CHUNK), CHUNK)

    def project(dy, h, m):
        rows = rows_of(m)
        total = jnp.dot(mix[0, rows], wts[dy, h, 0], preferred_element_type=F32)
        return total + jnp.dot(mix[1, rows], wts[dy, h, 1], preferred_element_type=F32)

    def to_y(dy):
        return dev(xh, z, k, (y + dy) % 4, xl)

    def far_copy(v, m):
        dy, h = unit_of(0, v)
        here = part.at[dy, h, rows_of(m)]
        return remote(here, got1.at[h, rows_of(m)], p_ss.at[dy, h, m], got1_rs.at[h, m], to_y(1 + 2 * (v % 2)))

    def near_copy(u, m):
        dy, h = unit_of(1, u)
        here = part.at[dy, h, rows_of(m)]
        there = got2.at[dy // 2, h, rows_of(m)]
        return remote(here, there, p_ss.at[dy, h, m], got2_rs.at[dy // 2, h, m], to_y(dy))

    def got1_wait(h, m):
        there = got1.at[h, rows_of(m)]
        remote(there, there, p_ss.at[0, h, m], got1_rs.at[h, m], yp).wait_recv()

    def got2_wait(side, h, m):
        there = got2.at[side, h, rows_of(m)]
        remote(there, there, p_ss.at[0, h, m], got2_rs.at[side, h, m], yp).wait_recv()

    def sib_wait(u):
        for kind in range(2):
            dy, h = unit_of(kind, u)
            for r in range(2):
                w_wait(dy, h, r, 1 - k)

    for s in range(4):
        relay(s, s + 1)
        sib_wait(s)
        mix_copy(chunk_at[s]).wait_recv()

        def early_body(n, _):
            u = jnp.minimum(n, s)
            m = NCHUNK - 1 - jnp.where(n <= s, s, n - s - 1)
            dy, h = unit_of(0, u)
            part[dy, h, rows_of(m)] = project(dy, h, m).astype(BF16)
            far_copy(u, m).start()
            dy, h = unit_of(1, u)
            part[dy, h, rows_of(m)] = project(dy, h, m).astype(BF16)
            near_copy(u, m).start()
            return 0

        lax.fori_loop(0, 2 * s + 1, early_body, 0)

    def late_step(u, _):
        relay(u, u + 1)
        sib_wait(u)

        def late_body(i, _):
            m = NCHUNK - 1 - i
            dy, h = unit_of(1, u)
            got1_wait(h, m)
            total = project(dy, h, m) + got1[h, rows_of(m)].astype(F32)
            part[dy, h, rows_of(m)] = total.astype(BF16)
            near_copy(u, m).start()
            dy, h = unit_of(0, u)
            part[dy, h, rows_of(m)] = project(dy, h, m).astype(BF16)
            return 0

        lax.fori_loop(0, NCHUNK, late_body, 0)
        return 0

    lax.fori_loop(4, 8, late_step, 0)

    for h in (0, 2, 1, 3):
        def sum_body(i, _):
            m = NCHUNK - 1 - i
            rows = rows_of(m)
            got2_wait(0, h, m)
            got2_wait(1, h, m)
            total = part[0, h, rows].astype(F32) + got2[0, h, rows].astype(F32) + got2[1, h, rows].astype(F32)
            total = total.astype(BF16)
            for core in range(2):
                out_ref[rows, pl.ds(core * 512 + h * LANES, LANES)] = total[:, core * LANES : (core + 1) * LANES]
            return 0

        lax.fori_loop(0, NCHUNK, sum_body, 0)

    halo_f.wait_send()
    halo_g.wait_send()
    for m in range(NCHUNK):
        mix_copy(m).wait_send()

    def sent_body(u, _):
        for kind in range(2):
            dy, h = unit_of(kind, u)
            for r in range(2):
                sib_copy(dy, h, r).wait_send()

        @pl.when(role == 0)
        def _():
            dy, h = unit_of(kind_here, u)
            for r in range(2):
                zp_copy(dy, h, r).wait_send()
                zm_copy(dy, h, r).wait_send()

        @pl.when(role == 1)
        def _():
            dya, ha = unit_of(kind_below, u)
            dyb, hb = unit_of(1 - kind_below, u)
            zp_copy(dya, ha, 0).wait_send()
            zm_copy(dyb, hb, 1).wait_send()

        for m in range(NCHUNK):
            near_copy(u, m).wait_send()
        return 0

    lax.fori_loop(0, 8, sent_body, 0)

    def far_sent_body(v, _):
        for m in range(NCHUNK):
            far_copy(v, m).wait_send()

        @pl.when(role == 0)
        def _():
            x_copy(v, 0, x2, 0).wait_send()

        @pl.when(role == 1)
        def _():
            x_copy(v, 1, xp, 0).wait_send()
            x_copy(v, 1, xn, 1).wait_send()

        return 0

    lax.fori_loop(0, 4, far_sent_body, 0)


def on_device(features, contig_starts, short_filter, medium_filter, filter_bias, out_weight):
    vmem = pl.BlockSpec(memory_space=pltpu.VMEM)
    hbm = pl.BlockSpec(memory_space=pl.ANY)
    dma = pltpu.SemaphoreType.DMA
    taps = medium_filter.astype(BF16).astype(F32)[:, ::-1]
    taps = jnp.concatenate([taps, jnp.zeros_like(taps)], axis=1)
    return pl.pallas_call(
        kernel,
        out_shape=jax.ShapeDtypeStruct((ROWS, CH), BF16),
        in_specs=[hbm, pl.BlockSpec(memory_space=pltpu.SMEM), vmem, vmem, vmem, hbm],
        out_specs=vmem,
        scratch_shapes=[
            pltpu.VMEM((3, HALO + ROWS, CH), BF16),
            pltpu.VMEM((3, 8 + BLK, CH), F32),
            pltpu.VMEM((NB + 1, BLK, CH), BF16),
            pltpu.VMEM((CH // GROUP, BLK, 2 * BLK), BF16),
            pltpu.VMEM((2 * BLK, 2 * LANES), BF16),
            pltpu.VMEM((BLK, 2 * LANES), F32),
            pltpu.VMEM((2, ROWS, CH), BF16),
            pltpu.VMEM((4, 4, 2, CH, 2 * LANES), BF16),
            pltpu.VMEM((4, 4, ROWS, 2 * LANES), BF16),
            pltpu.VMEM((4, ROWS, 2 * LANES), BF16),
            pltpu.VMEM((2, 4, ROWS, 2 * LANES), BF16),
            dma((3,)),
            dma((2,)),
            dma((2,)),
            dma((4, 4, 2, 2)),
            dma((4, 4, 2)),
            dma((4, 4, 2)),
            dma((4, 4, 2)),
            dma((4, 2)),
            dma((NCHUNK,)),
            dma((NCHUNK,)),
            dma((4, 4, NCHUNK)),
            dma((4, NCHUNK)),
            dma((2, 4, NCHUNK)),
        ],
        compiler_params=pltpu.CompilerParams(
            collective_id=0, has_side_effects=True, vmem_limit_bytes=60 * 1024 * 1024
        ),
        cost_estimate=pl.CostEstimate(
            flops=2 * ROWS * 2048 * 4096, bytes_accessed=16 * 1024 * 1024, transcendentals=0
        ),
    )(
        jnp.transpose(features, (1, 0, 2)),
        contig_starts,
        jnp.transpose(short_filter, (1, 0, 2)),
        taps,
        filter_bias.reshape(1, CH),
        out_weight,
    )


def solution(mesh):
    in_specs = (
        P("ctx", None, "tp"),
        P("ctx"),
        P(None, None, "tp"),
        P("tp", None),
        P("tp"),
        P("tp", "ctx"),
    )
    out_specs = P("ctx", "tp")
    return jax.shard_map(
        on_device, mesh=mesh, in_specs=in_specs, out_specs=out_specs, check_vma=False
    )
```

```python
import jax
import jax.numpy as jnp
from jax import lax
from jax.experimental import pallas as pl
from jax.experimental.pallas import tpu as pltpu
from jax.sharding import PartitionSpec as P

MESH = pl.DeviceIdType.MESH
F32 = jnp.float32
BF16 = jnp.bfloat16

ROWS = 1024
CH = 1024
BLK = 128
NB = ROWS // BLK
SPAN = 7
HALO = 16
GROUP = 16
LANES = 128
PER_TILE = LANES // GROUP
CHUNK = 256
NCHUNK = ROWS // CHUNK


TRANSFERS = (
    ((2, 0, 0, 0), (2, 0, 0, 0), (2, 0, 0, 0), (2, 0, 0, 0), (2, 1, 0, 0), (2, 1, 0, 0), (2, 1, 0, 0), (2, 1, 0, 0)),
    ((2, 0, 1, 0), (2, 0, 1, 0), (2, 0, 1, 0), (2, 0, 1, 0), (2, 1, 0, 0), (2, 1, 0, 0), (2, 1, 0, 0), (2, 1, 0, 0)),
    ((2, 0, 1, 0), (2, 0, 1, 0), (2, 0, 1, 0), (2, 0, 1, 0), (2, 1, 0, 0), (2, 1, 0, 0), (2, 1, 0, 0), (2, 1, 0, 0)),
    ((2, 0, 1, 0), (2, 0, 1, 0), (2, 0, 1, 0), (2, 0, 1, 0), (2, 1, 0, 0), (2, 1, 0, 0), (2, 1, 0, 0), (2, 1, 0, 0)),
    ((2, 1, 3, 0), (2, 1, 3, 0), (2, 1, 3, 0), (2, 1, 3, 0), (2, 3, 0, 0), (2, 3, 0, 0), (2, 3, 0, 0), (2, 3, 0, 0)),
    ((2, 1, 3, 0), (2, 1, 3, 0), (2, 1, 3, 0), (2, 1, 3, 0), (2, 3, 1, 1), (2, 3, 0, 1), (2, 3, 1, 1), (2, 3, 1, 0)),
    ((3, 1, 3, 0), (3, 1, 3, 0), (3, 1, 3, 0), (3, 1, 3, 0), (3, 3, 1, 1), (3, 3, 0, 1), (3, 3, 1, 1), (3, 3, 1, 0)),
    ((3, 2, 5, 0), (3, 2, 5, 0), (3, 2, 6, 0), (3, 2, 6, 0), (3, 5, 1, 1), (3, 5, 0, 1), (3, 5, 1, 1), (3, 5, 1, 0)),
    ((4, 2, 5, 0), (4, 2, 5, 0), (4, 2, 6, 0), (4, 2, 6, 0), (4, 5, 2, 2), (4, 5, 1, 2), (4, 5, 3, 2), (4, 5, 3, 0)),
    ((4, 3, 5, 0), (4, 3, 5, 0), (4, 3, 6, 0), (4, 3, 6, 0), (4, 5, 2, 2), (4, 5, 1, 2), (4, 5, 3, 2), (4, 5, 3, 0)),
    ((4, 3, 5, 0), (4, 3, 6, 0), (4, 3, 7, 0), (4, 3, 7, 0), (4, 5, 3, 4), (4, 5, 2, 4), (4, 5, 4, 3), (4, 5, 4, 2)),
    ((4, 3, 5, 0), (4, 3, 6, 0), (4, 3, 7, 0), (4, 3, 7, 0), (4, 5, 3, 4), (4, 5, 2, 4), (4, 5, 4, 3), (4, 5, 4, 2)),
    ((4, 4, 5, 0), (4, 4, 6, 0), (4, 4, 7, 0), (4, 4, 7, 0), (4, 5, 3, 4), (4, 5, 2, 4), (4, 5, 4, 3), (4, 5, 4, 2)),
    ((4, 4, 6, 2), (4, 4, 8, 0), (4, 4, 9, 0), (4, 4, 9, 0), (4, 5, 4, 5), (4, 5, 4, 4), (4, 5, 5, 4), (4, 5, 6, 2)),
    ((4, 4, 7, 4), (4, 4, 8, 4), (4, 4, 10, 2), (4, 4, 10, 2), (4, 7, 6, 6), (4, 7, 4, 8), (4, 7, 6, 6), (4, 7, 8, 4)),
    ((4, 4, 7, 6), (4, 4, 11, 4), (4, 4, 12, 4), (4, 4, 12, 4), (4, 7, 6, 8), (4, 7, 5, 8), (4, 7, 8, 6), (4, 7, 8, 4)),
    ((4, 4, 14, 6), (4, 4, 12, 6), (4, 4, 13, 4), (4, 4, 13, 4), (4, 7, 7, 9), (4, 7, 6, 9), (4, 7, 9, 7), (4, 7, 9, 6)),
    ((4, 4, 15, 8), (4, 4, 12, 6), (4, 4, 13, 6), (4, 4, 13, 4), (4, 8, 7, 10), (4, 8, 6, 10), (4, 8, 10, 7), (4, 8, 10, 6)),
    ((4, 4, 15, 8), (4, 4, 12, 8), (4, 4, 15, 6), (4, 4, 15, 6), (4, 8, 8, 11), (4, 8, 7, 12), (4, 8, 11, 8), (4, 8, 12, 6)),
    ((4, 4, 15, 9), (4, 4, 13, 8), (4, 4, 15, 6), (4, 4, 16, 6), (4, 8, 9, 12), (4, 8, 7, 12), (4, 8, 12, 9), (4, 8, 12, 7)),
    ((4, 4, 16, 9), (4, 4, 16, 10), (4, 4, 16, 7), (4, 4, 16, 6), (4, 8, 11, 12), (4, 8, 13, 13), (4, 8, 12, 11), (4, 8, 13, 13)),
    ((4, 4, 16, 10), (4, 4, 16, 10), (4, 4, 16, 7), (4, 4, 16, 7), (4, 8, 11, 13), (4, 8, 13, 13), (4, 8, 13, 11), (4, 8, 13, 13)),
    ((4, 4, 16, 10), (4, 4, 16, 10), (4, 4, 16, 8), (4, 4, 16, 8), (4, 8, 11, 13), (4, 8, 13, 13), (4, 8, 13, 11), (4, 8, 13, 13)),
    ((4, 4, 16, 10), (4, 4, 16, 10), (4, 4, 16, 10), (4, 4, 16, 8), (4, 8, 13, 13), (4, 8, 13, 13), (4, 8, 13, 13), (4, 8, 15, 14)),
    ((4, 4, 16, 10), (4, 4, 16, 12), (4, 4, 16, 10), (4, 4, 16, 10), (4, 8, 13, 15), (4, 8, 14, 15), (4, 8, 15, 13), (4, 8, 15, 14)),
    ((4, 4, 16, 12), (4, 4, 16, 12), (4, 4, 16, 12), (4, 4, 16, 10), (4, 8, 15, 16), (4, 8, 15, 16), (4, 8, 16, 15), (4, 8, 15, 14)),
    ((4, 4, 16, 12), (4, 4, 16, 12), (4, 4, 16, 12), (4, 4, 16, 12), (4, 8, 15, 16), (4, 8, 15, 16), (4, 8, 16, 15), (4, 8, 16, 15)),
    ((4, 4, 16, 12), (4, 4, 16, 13), (4, 4, 16, 14), (4, 4, 16, 12), (4, 8, 15, 16), (4, 8, 15, 16), (4, 8, 16, 15), (4, 8, 16, 15)),
    ((4, 4, 16, 13), (4, 4, 16, 13), (4, 4, 16, 16), (4, 4, 16, 14), (4, 8, 16, 16), (4, 8, 16, 16), (4, 8, 16, 16), (4, 8, 16, 16)),
    ((4, 4, 16, 14), (4, 4, 16, 14), (4, 4, 16, 16), (4, 4, 16, 16), (4, 8, 16, 16), (4, 8, 16, 16), (4, 8, 16, 16), (4, 8, 16, 16)),
    ((4, 4, 16, 14), (4, 4, 16, 14), (4, 4, 16, 16), (4, 4, 16, 16), (4, 8, 16, 16), (4, 8, 16, 16), (4, 8, 16, 16), (4, 8, 16, 16)),
    ((4, 4, 16, 16), (4, 4, 16, 16), (4, 4, 16, 16), (4, 4, 16, 16), (4, 8, 16, 16), (4, 8, 16, 16), (4, 8, 16, 16), (4, 8, 16, 16)),
    ((4, 4, 16, 16), (4, 4, 16, 16), (4, 4, 16, 16), (4, 4, 16, 16), (4, 8, 16, 16), (4, 8, 16, 16), (4, 8, 16, 16), (4, 8, 16, 16)),
)
PHASES = (
    (
        ((0, 1), 1, (3, 7)),
        ((0, 4), 1, (3, 19)),
        ((8, 9), 1, (35, 39)),
        ((8, 9), 1, (35, 39)),
        ((0, 8), 1, (3, 35)),
        ((0, 8), 1, (3, 35)),
        ((0, 8), 1, (3, 35)),
        ((0, 8), 1, (3, 35)),
    ),
    (
        ((2, 8), 0, (11, 35)),
        ((1, 5), 0, (7, 23)),
        ((10, 11), 0, (43, 47)),
        ((10, 11), 0, (43, 47)),
        ((9, 1), 0, (39, 7)),
        ((9, 1), 0, (39, 7)),
        ((9, 1), 0, (39, 7)),
        ((9, 10), 0, (39, 43)),
    ),
    (
        ((9,), 1, (39, 2, 6, 10, 34)),
        ((8, 9), 0, (35, 39)),
        ((12, 0), 0, (51, 3)),
        ((12, 0), 0, (51, 3)),
        ((10, 2), 0, (43, 11)),
        ((10, 11), 0, (43, 47)),
        ((10, 2), 0, (43, 11)),
        ((1, 11), 0, (7, 47)),
    ),
    (
        ((10,), 0, (38, 43, 42)),
        ((2,), 1, (11, 2, 18, 6, 22)),
        ((1, 13), 0, (7, 55)),
        ((13, 1), 0, (55, 7)),
        ((11,), 1, (47, 2, 34, 38, 6)),
        ((), 1, (2, 34, 38, 6, 42)),
        ((11,), 1, (47, 2, 34, 38, 6)),
        ((), 1, (2, 34, 38, 42, 6)),
    ),
    (
        ((3,), 0, (15, 14)),
        ((), 0, (34, 38, 10)),
        ((), 1, (34, 38, 42, 46, 2)),
        ((), 1, (34, 38, 42, 46, 2)),
        ((), 0, (42, 10, 46)),
        ((2,), 0, (46, 11, 10)),
        ((), 0, (42, 10, 46)),
        ((2,), 0, (46, 11, 10)),
    ),
    (
        ((4,), 0, (19, 18)),
        ((10,), 0, (43, 42)),
        ((), 0, (6, 50)),
        ((), 0, (6, 50, 54)),
        ((12,), 0, (51, 50)),
        ((12,), 0, (51, 50)),
        ((12,), 0, (51, 50)),
        ((12,), 0, (51, 50)),
    ),
    (
        ((5,), 0, (23, 22)),
        ((11,), 0, (47, 46)),
        ((2,), 0, (11, 10, 54)),
        ((2,), 0, (11, 10)),
        ((3,), 0, (15, 14)),
        ((13,), 0, (55, 54)),
        ((3,), 0, (15, 14)),
        ((13,), 0, (55, 54)),
    ),
    (
        ((6,), 0, (27, 26)),
        ((3,), 0, (15, 14)),
        ((14,), 0, (59, 58)),
        ((14,), 0, (59, 58)),
        ((13,), 0, (55, 54)),
        ((), 1, (1, 33, 37, 5, 41)),
        ((13,), 0, (55, 54)),
        ((), 1, (1, 33, 37, 41, 5)),
    ),
    (
        ((11,), 0, (47, 46)),
        ((6,), 0, (27, 26)),
        ((15,), 1, (63, 33, 37, 41, 45)),
        ((15,), 1, (63, 33, 37, 41, 45)),
        ((), 1, (1, 33, 37, 5, 41)),
        ((), 0, (45, 9)),
        ((), 1, (1, 33, 37, 5, 41)),
        ((), 0, (45, 9)),
    ),
    (
        ((7,), 0, (31, 30)),
        ((7,), 0, (31, 30)),
        ((), 0, (1, 5, 9, 62)),
        ((), 0, (1, 5, 9, 62, 49)),
        ((), 0, (9, 45, 13)),
        ((3,), 0, (15, 14, 13)),
        ((), 0, (9, 45, 13)),
        ((3,), 0, (15, 14, 13)),
    ),
    (
        ((12,), 0, (51, 50)),
        ((12,), 0, (51, 50)),
        ((3,), 0, (15, 14, 13, 53, 49)),
        ((3,), 0, (15, 14, 13)),
        ((4,), 0, (19, 18, 17)),
        ((4,), 0, (19, 18, 17)),
        ((4,), 0, (19, 18, 17)),
        ((4,), 0, (19, 18, 17)),
    ),
    (
        ((), 1, (1, 5, 9, 33, 37)),
        ((), 1, (1, 17, 5, 21, 33)),
        ((4,), 0, (57, 19, 18, 17)),
        ((), 1, (32, 36, 40, 44, 0)),
        ((5,), 0, (23, 22, 21)),
        ((5,), 0, (23, 22, 21, 49, 53)),
        ((5,), 0, (23, 22, 21)),
        ((5,), 0, (23, 22, 21, 53, 49)),
    ),
    (
        ((), 0, (41, 13, 17, 21, 25)),
        ((), 0, (37, 9, 41, 45, 13)),
        ((), 1, (32, 36, 40, 44, 0)),
        ((), 0, (4, 8, 12, 53, 57)),
        ((14,), 0, (59, 58, 53)),
        ((6,), 0, (27, 26, 25)),
        ((14,), 0, (59, 58, 53)),
        ((14,), 0, (59, 58)),
    ),
    (
        ((), 0, (45, 29)),
        ((), 0, (25, 29)),
        ((), 0, (4, 8, 12, 16, 61)),
        ((4,), 0, (19, 18, 17, 16, 61)),
        ((), 1, (0, 32, 36, 4, 40)),
        ((14,), 0, (59, 58)),
        ((), 1, (0, 32, 36, 4, 40)),
        ((6,), 0, (27, 26, 25)),
    ),
    (
        ((13,), 0, (55, 54)),
        ((13,), 0, (55, 54)),
        ((5,), 0, (23, 22, 21, 20)),
        ((5,), 0, (48, 23, 22, 21, 20)),
        ((), 0, (8, 44, 12, 16, 20)),
        ((), 1, (0, 32, 36, 4, 40)),
        ((), 0, (8, 44, 12, 16, 20)),
        ((), 1, (0, 32, 36, 40, 4)),
    ),
    (
        ((), 1, (0, 4, 8, 32, 36)),
        ((), 1, (0, 16, 4, 20, 32)),
        ((6,), 0, (27, 26, 25, 24, 52)),
        ((), 0, (52, 56)),
        ((6,), 0, (49, 27, 26, 25, 24)),
        ((), 0, (44, 8, 12, 16, 20)),
        ((6,), 0, (49, 27, 26, 25, 24)),
        ((), 0, (44, 8, 12, 16, 20)),
    ),
    (
        ((), 0, (40, 12, 16, 20, 24)),
        ((), 0, (36, 8, 40, 44, 12)),
        ((7,), 0, (48, 31, 30, 29, 28)),
        ((6,), 0, (27, 26, 25, 24, 60)),
        ((15,), 0, (63, 62, 57, 61)),
        ((), 0, (24, 57)),
        ((15,), 0, (63, 62, 57, 61)),
        ((), 0, (24, 57)),
    ),
    (
        ((), 0, (44, 28, 53, 49)),
        ((), 0, (24, 28, 49, 53)),
        ((), 0, (56, 60)),
        ((7,), 0, (31, 30, 29, 28)),
        ((7,), 0, (31, 30, 29, 28, 48)),
        ((15,), 0, (63, 62, 61)),
        ((7,), 0, (31, 30, 29, 28, 48)),
        ((15,), 0, (63, 62, 61)),
    ),
    (
        ((14,), 0, (59, 58, 57)),
        ((14,), 0, (59, 58, 57)),
        ((), 0, ()),
        ((), 0, ()),
        ((), 0, (52, 56, 60)),
        ((7,), 0, (31, 30, 29, 28, 48)),
        ((), 0, (52, 56, 60)),
        ((7,), 0, (31, 30, 29, 28, 48)),
    ),
    (
        ((15,), 0, (63, 62, 61, 52, 60)),
        ((15,), 0, (63, 62, 61, 48, 52)),
        ((), 0, ()),
        ((), 0, ()),
        ((), 0, ()),
        ((), 0, (52, 56, 60)),
        ((), 0, ()),
        ((), 0, (52, 56, 60)),
    ),
    (
        ((), 0, (48, 56)),
        ((), 0, (56, 60)),
        ((), 0, ()),
        ((), 0, ()),
        ((), 0, ()),
        ((), 0, ()),
        ((), 0, ()),
        ((), 0, ()),
    ),
)


def quarter(dy, i):
    odd = dy % 2
    return (1 - odd) * (2 * (i % 2) + i // 2) + odd * ((i + 3 - dy) % 4)


def kernel(
    feats, starts, sw, rtaps, bias, w_ref, out_ref,
    passing, fbuf, ext, gbuf, toep, xs, conv, mix, wts, part, got1, got2,
    f_sem, halo_ss, halo_rs, pass_rs, pass_ss, zx_ss, w_rs, sib_ss, zp_ss, zm_ss, x_ss, mix_ss, mix_rs,
    p_ss, got1_rs, got2_rs,
):
    c, t = lax.axis_index("ctx"), lax.axis_index("tp")
    xh, z, k = c // 8, (c // 2) % 4, c % 2
    y, xl = t // 2, t % 2
    role = (xl + z) % 2

    def dev(xh, z, k, y, xl):
        return ((xh * 4 + z) * 2 + k, y * 2 + xl)

    sib = dev(xh, z, 1 - k, y, xl)
    zp, zm = dev(xh, (z + 1) % 4, k, y, xl), dev(xh, (z + 3) % 4, k, y, xl)
    yp, ym = dev(xh, z, k, (y + 1) % 4, xl), dev(xh, z, k, (y + 3) % 4, xl)
    xp, xn = dev(xh, z, k, y, 1 - xl), dev(1 - xh, z, k, y, 1 - xl)
    nxt, prv = ((c + 1) % 16, t), ((c + 15) % 16, t)

    f_copies = []
    for s in range(3):
        cp = pltpu.make_async_copy(feats.at[s], fbuf.at[s, pl.ds(HALO, ROWS)], f_sem.at[s])
        cp.start()
        f_copies.append(cp)

    barrier = pltpu.get_barrier_semaphore()
    for d in (sib, zp, zm, yp, ym, xp, xn, prv):
        pl.semaphore_signal(barrier, inc=1, device_id=d, device_id_type=MESH)
    pl.semaphore_wait(barrier, 8)

    def remote(src, dst, ss, rs, d):
        return pltpu.make_async_remote_copy(
            src_ref=src, dst_ref=dst, send_sem=ss, recv_sem=rs, device_id=d, device_id_type=MESH
        )

    dy_own = (2 * xh + z // 2 - y + 4) % 4

    def w_piece(h):
        return w_ref.at[:, pl.ds(h * LANES, LANES)]

    def slot(dy, h, r, core):
        return wts.at[dy, h, r, :, pl.ds(pl.multiple_of(core * LANES, LANES), LANES)]

    def x_copy(i, side):
        h = quarter(dy_own, i)
        return remote(
            w_piece(h), slot(dy_own, h, 1, k), x_ss.at[i, side], w_rs.at[dy_own, h, 1, k], (xp, xn)[side]
        )

    def pass_copy(i):
        h = quarter(dy_own, i)
        return remote(w_piece(h), passing.at[i], x_ss.at[i, 0], pass_rs.at[i], xp)

    def z_pass_copy(i, side):
        h = quarter(dy_own, i)
        return remote(
            w_piece(h), passing.at[4 * side + i], zx_ss.at[i, side], pass_rs.at[4 * side + i], (zp, zm)[side]
        )

    def z_onward_copy(i, side):
        dy = (2 * xh + ((z + 3 + 2 * side) % 4) // 2 - y + 4) % 4
        h = quarter(dy, i)
        return remote(
            passing.at[4 * side + i], slot(dy, h, 1, k), pass_ss.at[4 * side + i], w_rs.at[dy, h, 1, k], xn
        )

    def onward_copy(i):
        h = quarter(dy_own, i)
        return remote(passing.at[i], slot(dy_own, h, 0, k), pass_ss.at[i], w_rs.at[dy_own, h, 0, k], xn)

    halo_f = remote(
        feats.at[:, pl.ds(ROWS - HALO, HALO)], fbuf.at[:, pl.ds(0, HALO)], halo_ss.at[0], halo_rs.at[0], nxt
    )
    halo_f.start()

    @pl.when(role == 0)
    def _():
        for i in range(4):
            h = quarter(dy_own, i)
            pltpu.make_async_copy(w_piece(h), slot(dy_own, h, 0, k), w_rs.at[dy_own, h, 0, k]).start()

    @pl.when(role == 1)
    def _():
        for i in range(4):
            z_pass_copy(i, 0).start()
            z_pass_copy(i, 1).start()

    def sib_copy(dy, h, r):
        here = slot(dy, h, r, k)
        return remote(here, here, sib_ss.at[dy, h, r], w_rs.at[dy, h, r, k], sib)

    def zp_copy(dy, h, r):
        here = slot(dy, h, r, k)
        return remote(here, here, zp_ss.at[dy, h, r], w_rs.at[dy, h, r, k], zp)

    def zm_copy(dy, h, r):
        here = slot(dy, h, r, k)
        return remote(here, here, zm_ss.at[dy, h, r], w_rs.at[dy, h, r, k], zm)

    def w_wait(dy, h, r, core):
        here = slot(dy, h, r, core)
        remote(here, here, sib_ss.at[dy, h, r], w_rs.at[dy, h, r, core], sib).wait_recv()

    kind_here = (z // 2 + y) % 2
    kind_below = (((z + 3) % 4) // 2 + y) % 2
    first_odd = 1 + 2 * ((((y + 1) % 4) // 2 + xh) % 2)

    def unit_of(kind, u):
        dy0, i0 = 2 - 2 * (u // 4), u % 4
        odd = u % 2
        dy1, i1 = first_odd * (1 - odd) + (4 - first_odd) * odd, u // 2
        dy, i = dy0 + kind * (dy1 - dy0), i0 + kind * (i1 - i0)
        return dy, quarter(dy, i)

    def side_of(dy):
        return (((y + dy) % 4) // 2 + xh) % 2

    def piece_of(kind, n):
        dy, h = unit_of(kind, n // 2)
        return dy, h, (n + side_of(dy)) % 2

    near_far = [(0, 0), (1, 0), (0, 1), (1, 1), (0, 2), (1, 2), (0, 3), (1, 3)]
    near_far += [(t, i) for i in range(4) for t in (3, 2)]
    far_far = [(0, 0), (1, 0), (3, 0), (2, 0), (0, 1), (3, 1), (2, 1), (1, 1)]
    far_far += [(3, 2), (2, 2), (0, 2), (3, 3), (2, 3), (1, 2), (0, 3), (1, 3)]
    mixed = [(t, i) for i in range(4) for t in (0, 1, 3, 2)]
    far_side = side_of(2)
    kind = kind_here + role * (kind_below - kind_here)
    cls = role * 4 + kind * 2 + far_side

    def pick(values):
        a, b, c2, d = values
        if a == b == c2 == d:
            return a
        return a + far_side * (b - a) + kind * (c2 - a) + kind * far_side * (d - c2 - b + a)

    def pick_any(values):
        if all(v == values[0] for v in values):
            return values[0]
        picked = jnp.int32(values[0])
        for n in range(1, 8):
            picked = jnp.where(cls == n, jnp.int32(values[n]), picked)
        return picked

    def xp_step(n):
        @pl.when(role == 0)
        def _():
            pass_copy(n).start()

        @pl.when(role == 1)
        def _():
            x_copy(n, 0).start()

    def z_onward_step(n):
        for side in range(2):
            z_pass_copy(n, side).wait_recv()
            z_onward_copy(n, side).start()

    def spread_step(n):
        code = jnp.int32(0)
        for m in range(16):
            choices = [t * 4 + i for t, i in (near_far[m], far_far[m], mixed[m], mixed[m])]
            code = jnp.where(n == m, pick(choices), code)
        t, i = code // 4, code % 4
        dy = (dy_own + 2 * (t // 2)) % 4
        h, r = quarter(dy, i), t % 2
        w_wait(dy, h, r, k)

        @pl.when(t != 3)
        def _():
            zp_copy(dy, h, r).start()
            zm_copy(dy, h, r).start()

        sib_copy(dy, h, r).start()

    def relay_step(n):
        dy, h, r = piece_of(1 - kind_here, n)
        w_wait(dy, h, r, k)
        sib_copy(dy, h, r).start()

    def xn_step(n):
        i = n // 2

        @pl.when(n % 2 == 0)
        def _():
            x_copy(i, 1).start()

        @pl.when(n % 2 == 1)
        def _():
            pass_copy(i).wait_recv()
            onward_copy(i).start()

    def from_below_step(n):
        dy, h, r = piece_of(kind_below, n)
        w_wait(dy, h, r, k)

        @pl.when(r == 0)
        def _():
            zp_copy(dy, h, r).start()

        sib_copy(dy, h, r).start()

    def from_above_step(n):
        dy, h, r = piece_of(1 - kind_below, n)
        w_wait(dy, h, r, k)

        @pl.when(r == 1)
        def _():
            zm_copy(dy, h, r).start()

        sib_copy(dy, h, r).start()

    sequences = (
        (xp_step, z_onward_step, spread_step, relay_step),
        (xp_step, xn_step, from_below_step, from_above_step),
    )

    def transfers(point):
        for r in range(2):
            now = TRANSFERS[point][4 * r : 4 * r + 4]
            then = TRANSFERS[point - 1][4 * r : 4 * r + 4] if point else ((0,) * 4,) * 4
            if now == then:
                continue

            @pl.when(role == r)
            def _():
                for q, step in enumerate(sequences[r]):
                    lo, hi = [v[q] for v in then], [v[q] for v in now]
                    if lo != hi:
                        def body(n, _, step=step):
                            step(n)
                            return 0

                        lax.fori_loop(pick(lo), pick(hi), body, 0)

    def toep_body(g, _):
        row = jnp.broadcast_to(rtaps[pl.ds(g, 1)], (BLK, 2 * BLK))
        toep[g] = pltpu.roll(row, 1, 1, stride=1, stride_axis=0).astype(BF16)
        return 0

    transfers(0)
    lax.fori_loop(0, CH // GROUP // 2, toep_body, 0)
    transfers(1)
    lax.fori_loop(CH // GROUP // 2, CH // GROUP, toep_body, 0)
    transfers(2)

    first = (c > 0).astype(F32)

    def keep_of(b):
        kept = (1 - starts[b]).astype(F32)
        return kept * jnp.where(b == 0, first, 1.0)

    def short(s, b, keep, lanes):
        tail = fbuf[s, pl.ds(pl.multiple_of(b * BLK, BLK), HALO), lanes].astype(F32)
        ext[s, pl.ds(0, 8), lanes] = tail[8:] * keep
        ext[s, pl.ds(8, BLK), lanes] = fbuf[
            s, pl.ds(pl.multiple_of(b * BLK + HALO, HALO), BLK), lanes
        ].astype(F32)
        total = sw[s, pl.ds(0, 1), lanes] * ext[s, pl.ds(8, BLK), lanes]
        for j in range(1, SPAN):
            total += sw[s, pl.ds(j, 1), lanes] * ext[s, pl.ds(8 - j, BLK), lanes]
        return total

    def lanes_of(lt):
        return pl.ds(pl.multiple_of(lt * LANES, LANES), LANES)

    def gate(b):
        keep = keep_of(b)

        def body(lt, _):
            lanes = lanes_of(lt)
            gbuf[b + 1, :, lanes] = (short(1, b, keep, lanes) * short(2, b, keep, lanes)).astype(BF16)
            return 0

        lax.fori_loop(0, CH // LANES, body, 0)

    def mix_copy(m):
        rows = pl.ds(m * CHUNK, CHUNK)
        return remote(mix.at[0, rows], mix.at[1, rows], mix_ss.at[m], mix_rs.at[m], xp)

    lane_group = lax.broadcasted_iota(jnp.int32, (BLK, 2 * LANES), 1) % LANES // GROUP

    def mix_pair(b0, lo, hi):
        keeps = [keep_of(b0), keep_of(b0 + 1)]

        def body(lt, _):
            lanes = lanes_of(lt)
            for i in range(2):
                cols = pl.ds(i * LANES, LANES)
                xs[pl.ds(0, BLK), cols] = (gbuf[b0 + i, :, lanes].astype(F32) * keeps[i]).astype(BF16)
                xs[pl.ds(BLK, BLK), cols] = gbuf[b0 + i + 1, :, lanes]
            mats = toep[pl.ds(lt * PER_TILE, PER_TILE)].reshape(PER_TILE * BLK, 2 * BLK)
            every = jnp.dot(mats, xs[...], preferred_element_type=F32)
            every = every.reshape(PER_TILE, BLK, 2 * LANES)
            picked = every[0]
            for g in range(1, PER_TILE):
                picked = jnp.where(lane_group == g, every[g], picked)
            conv[...] = picked
            for i in range(2):
                gated = gbuf[b0 + i + 1, :, lanes].astype(F32)
                query = short(0, b0 + i, keeps[i], lanes)
                direct = conv[:, pl.ds(i * LANES, LANES)] + bias[:, lanes] * gated
                mix[0, pl.ds(pl.multiple_of((b0 + i) * BLK, BLK), BLK), lanes] = (query * direct).astype(BF16)
            return 0

        lax.fori_loop(lo, hi, body, 0)

    chunk_at = [NCHUNK - 1 - i for i in range(NCHUNK)]

    tiles = CH // LANES
    for cp in f_copies:
        cp.wait()
    gate(NB - 1)
    halo_g = remote(gbuf.at[NB], gbuf.at[0], halo_ss.at[1], halo_rs.at[1], nxt)
    halo_g.start()
    transfers(3)
    point = 4
    for m in chunk_at:
        if m > 0:
            gate(2 * m)
            gate(2 * m - 1)
        else:
            halo_f.wait_recv()
            gate(0)
            halo_g.wait_recv()
        transfers(point)
        point += 1
        if m == NCHUNK - 1:
            mix_pair(2 * m, 0, tiles // 2)
            transfers(point)
            point += 1
            mix_pair(2 * m, tiles // 2, tiles)
        else:
            mix_pair(2 * m, 0, tiles)
        mix_copy(m).start()
        transfers(point)
        point += 1

    def rows_of(m):
        return pl.ds(pl.multiple_of(m * CHUNK, CHUNK), CHUNK)

    def project(dy, h, m):
        rows = rows_of(m)
        total = jnp.dot(mix[0, rows], wts[dy, h, 0], preferred_element_type=F32)
        return total + jnp.dot(mix[1, rows], wts[dy, h, 1], preferred_element_type=F32)

    def to_y(dy):
        return dev(xh, z, k, (y + dy) % 4, xl)

    def far_copy(v, m):
        dy, h = 2, quarter(2, v)
        here = part.at[dy, h, rows_of(m)]
        return remote(here, got1.at[h, rows_of(m)], p_ss.at[dy, h, m], got1_rs.at[h, m], to_y(1 + 2 * (v % 2)))

    def near_copy(u, m):
        dy, h = unit_of(1, u)
        here = part.at[dy, h, rows_of(m)]
        there = got2.at[dy // 2, h, rows_of(m)]
        return remote(here, there, p_ss.at[dy, h, m], got2_rs.at[dy // 2, h, m], to_y(dy))

    def got1_wait(h, m):
        there = got1.at[h, rows_of(m)]
        remote(there, there, p_ss.at[0, h, m], got1_rs.at[h, m], yp).wait_recv()

    def got2_wait(side, h, m):
        there = got2.at[side, h, rows_of(m)]
        remote(there, there, p_ss.at[0, h, m], got2_rs.at[side, h, m], yp).wait_recv()

    def tile_step(_, packed):
        code = packed % 64
        knd, u, m = code // 32, code // 4 % 8, code % 4
        dy, h = unit_of(knd, u)
        rows = rows_of(m)
        total = project(dy, h, m)
        depends = (knd == 1) & (u >= 4)

        @pl.when(depends)
        def _():
            got1_wait(h, m)
            part[dy, h, rows] = (total + got1[h, rows].astype(F32)).astype(BF16)

        @pl.when(jnp.logical_not(depends))
        def _():
            part[dy, h, rows] = total.astype(BF16)

        @pl.when((knd == 0) & (u < 4))
        def _():
            far_copy(u, m).start()

        @pl.when(knd == 1)
        def _():
            near_copy(u, m).start()

        return packed // 64

    chunks = [0] * 8
    for p, phase in enumerate(PHASES):
        if p:
            transfers(point)
            point += 1
        for n, (waits, _, _) in enumerate(phase):
            if waits:
                @pl.when(cls == n)
                def _():
                    for code in waits:
                        dy, h = unit_of(code // 8, code % 8)
                        for r in range(2):
                            w_wait(dy, h, r, 1 - k)

        before = list(chunks)
        chunks = [a + row[1] for a, row in zip(chunks, phase)]
        if before != chunks:
            def chunk_step(n, _):
                mix_copy(NCHUNK - 1 - n).wait_recv()
                return 0

            lax.fori_loop(pick_any(before), pick_any(chunks), chunk_step, 0)
        packed = [sum(code * 64**n for n, code in enumerate(row[2])) for row in phase]
        lax.fori_loop(0, pick_any([len(row[2]) for row in phase]), tile_step, pick_any(packed) + jnp.int32(0))

    for h in (0, 2, 1, 3):
        def sum_body(i, _):
            m = NCHUNK - 1 - i
            rows = rows_of(m)
            got2_wait(0, h, m)
            got2_wait(1, h, m)
            total = part[0, h, rows].astype(F32) + got2[0, h, rows].astype(F32) + got2[1, h, rows].astype(F32)
            total = total.astype(BF16)
            for core in range(2):
                out_ref[rows, pl.ds(core * 512 + h * LANES, LANES)] = total[:, core * LANES : (core + 1) * LANES]
            return 0

        lax.fori_loop(0, NCHUNK, sum_body, 0)

    halo_f.wait_send()
    halo_g.wait_send()
    for m in range(NCHUNK):
        mix_copy(m).wait_send()

    def sent_body(u, _):
        for kind in range(2):
            dy, h = unit_of(kind, u)
            for r in range(2):
                sib_copy(dy, h, r).wait_send()

        @pl.when(role == 1)
        def _():
            dya, ha = unit_of(kind_below, u)
            dyb, hb = unit_of(1 - kind_below, u)
            zp_copy(dya, ha, 0).wait_send()
            zm_copy(dyb, hb, 1).wait_send()

        for m in range(NCHUNK):
            near_copy(u, m).wait_send()
        return 0

    lax.fori_loop(0, 8, sent_body, 0)

    def far_sent_body(v, _):
        for m in range(NCHUNK):
            far_copy(v, m).wait_send()

        @pl.when(role == 0)
        def _():
            pass_copy(v).wait_send()
            for t in range(3):
                dy = (dy_own + 2 * (t // 2)) % 4
                zp_copy(dy, quarter(dy, v), t % 2).wait_send()
                zm_copy(dy, quarter(dy, v), t % 2).wait_send()
            z_onward_copy(v, 0).wait_send()
            z_onward_copy(v, 1).wait_send()

        @pl.when(role == 1)
        def _():
            x_copy(v, 0).wait_send()
            x_copy(v, 1).wait_send()
            onward_copy(v).wait_send()
            z_pass_copy(v, 0).wait_send()
            z_pass_copy(v, 1).wait_send()

        return 0

    lax.fori_loop(0, 4, far_sent_body, 0)


def on_device(features, contig_starts, short_filter, medium_filter, filter_bias, out_weight):
    vmem = pl.BlockSpec(memory_space=pltpu.VMEM)
    hbm = pl.BlockSpec(memory_space=pl.ANY)
    dma = pltpu.SemaphoreType.DMA
    taps = medium_filter.astype(BF16).astype(F32)[:, ::-1]
    taps = jnp.concatenate([taps, jnp.zeros_like(taps)], axis=1)
    return pl.pallas_call(
        kernel,
        out_shape=jax.ShapeDtypeStruct((ROWS, CH), BF16),
        in_specs=[hbm, pl.BlockSpec(memory_space=pltpu.SMEM), vmem, vmem, vmem, hbm],
        out_specs=vmem,
        scratch_shapes=[
            pltpu.VMEM((8, CH, LANES), BF16),
            pltpu.VMEM((3, HALO + ROWS, CH), BF16),
            pltpu.VMEM((3, 8 + BLK, CH), F32),
            pltpu.VMEM((NB + 1, BLK, CH), BF16),
            pltpu.VMEM((CH // GROUP, BLK, 2 * BLK), BF16),
            pltpu.VMEM((2 * BLK, 2 * LANES), BF16),
            pltpu.VMEM((BLK, 2 * LANES), F32),
            pltpu.VMEM((2, ROWS, CH), BF16),
            pltpu.VMEM((4, 4, 2, CH, 2 * LANES), BF16),
            pltpu.VMEM((4, 4, ROWS, 2 * LANES), BF16),
            pltpu.VMEM((4, ROWS, 2 * LANES), BF16),
            pltpu.VMEM((2, 4, ROWS, 2 * LANES), BF16),
            dma((3,)),
            dma((2,)),
            dma((2,)),
            dma((8,)),
            dma((8,)),
            dma((4, 2)),
            dma((4, 4, 2, 2)),
            dma((4, 4, 2)),
            dma((4, 4, 2)),
            dma((4, 4, 2)),
            dma((4, 2)),
            dma((NCHUNK,)),
            dma((NCHUNK,)),
            dma((4, 4, NCHUNK)),
            dma((4, NCHUNK)),
            dma((2, 4, NCHUNK)),
        ],
        compiler_params=pltpu.CompilerParams(
            collective_id=0, has_side_effects=True, vmem_limit_bytes=60 * 1024 * 1024
        ),
        cost_estimate=pl.CostEstimate(
            flops=2 * ROWS * 2048 * 4096, bytes_accessed=16 * 1024 * 1024, transcendentals=0
        ),
    )(
        jnp.transpose(features, (1, 0, 2)),
        contig_starts,
        jnp.transpose(short_filter, (1, 0, 2)),
        taps,
        filter_bias.reshape(1, CH),
        out_weight,
    )


def solution(mesh):
    in_specs = (
        P("ctx", None, "tp"),
        P("ctx"),
        P(None, None, "tp"),
        P("tp", None),
        P("tp"),
        P("tp", "ctx"),
    )
    out_specs = P("ctx", "tp")
    return jax.shard_map(
        on_device, mesh=mesh, in_specs=in_specs, out_specs=out_specs, check_vma=False
    )
```

```python
import jax
import jax.numpy as jnp
from jax import lax
from jax.experimental import pallas as pl
from jax.experimental.pallas import tpu as pltpu
from jax.sharding import PartitionSpec as P

MESH = pl.DeviceIdType.MESH
F32 = jnp.float32
BF16 = jnp.bfloat16

ROWS = 1024
CH = 1024
BLK = 128
NB = ROWS // BLK
SPAN = 7
HALO = 16
GROUP = 16
OUT = jnp.bfloat16
LANES = 128
PER_TILE = LANES // GROUP
CHUNK = 256
NCHUNK = ROWS // CHUNK


ORDERS = (
    ((0, 4, 1, 5, 6, 2, 3, 7, 8, 14, 13, 9, 12, 10, 15, 11), (3, 1, 0, 2, 4, 5, 7, 6, 9, 10, 11, 8, 13, 12, 15, 14)),
    ((0, 1, 12, 8, 4, 9, 5, 13, 14, 10, 2, 15, 11, 6, 3, 7), (0, 1, 3, 2, 4, 6, 5, 7, 10, 9, 8, 11, 14, 15, 12, 13)),
    ((0, 4, 5, 12, 8, 1, 13, 9, 2, 14, 6, 10, 7, 15, 3, 11), (2, 0, 3, 1, 4, 5, 10, 7, 6, 8, 9, 11, 12, 13, 15, 14)),
    ((0, 1, 4, 8, 13, 5, 12, 9, 2, 14, 6, 10, 15, 3, 7, 11), (1, 0, 2, 3, 4, 5, 6, 11, 8, 7, 12, 9, 15, 10, 14, 13)),
    ((0, 2, 1, 3, 5, 10, 8, 4, 12, 6, 7, 9, 11, 14, 13, 15), (2, 1, 3, 0, 5, 6, 4, 7, 8, 9, 10, 11, 13, 14, 15, 12)),
    ((0, 1, 9, 2, 3, 5, 4, 8, 6, 7, 10, 11, 12, 14, 13, 15), (0, 1, 2, 3, 5, 6, 7, 4, 9, 10, 8, 11, 14, 13, 15, 12)),
    ((0, 2, 1, 3, 5, 6, 4, 7, 10, 8, 9, 11, 14, 13, 12, 15), (0, 1, 2, 3, 4, 5, 6, 10, 7, 8, 12, 9, 13, 11, 14, 15)),
    ((0, 1, 3, 2, 4, 5, 7, 6, 8, 9, 11, 10, 12, 15, 13, 14), (1, 0, 2, 3, 4, 5, 10, 11, 6, 8, 7, 12, 9, 14, 15, 13)),
)
TRANSFERS = (
    ((1, 0, 0, 0), (1, 0, 0, 0), (2, 0, 1, 0), (2, 0, 0, 0), (1, 1, 1, 0, 0), (2, 1, 0, 0, 0), (1, 2, 1, 0, 0), (2, 1, 0, 0, 0)),
    ((2, 0, 1, 0), (1, 0, 0, 0), (2, 0, 1, 0), (3, 0, 1, 0), (1, 1, 1, 0, 0), (2, 1, 0, 0, 0), (1, 3, 1, 0, 0), (2, 2, 0, 0, 0)),
    ((2, 0, 1, 0), (2, 0, 0, 0), (3, 0, 1, 0), (3, 0, 1, 0), (3, 2, 1, 0, 0), (2, 2, 0, 0, 0), (3, 3, 1, 0, 0), (2, 2, 0, 0, 0)),
    ((2, 0, 1, 0), (3, 0, 1, 0), (3, 0, 1, 0), (3, 0, 2, 0), (3, 2, 1, 0, 0), (2, 2, 1, 0, 0), (3, 3, 3, 0, 0), (2, 2, 1, 0, 0)),
    ((2, 0, 2, 0), (3, 1, 2, 0), (3, 1, 2, 0), (3, 0, 3, 0), (3, 2, 1, 0, 0), (2, 4, 2, 0, 0), (3, 3, 3, 0, 0), (3, 3, 2, 0, 0)),
    ((2, 0, 3, 0), (3, 1, 2, 0), (3, 1, 3, 0), (3, 2, 4, 0), (3, 2, 3, 0, 0), (2, 4, 3, 0, 0), (3, 4, 3, 0, 0), (3, 4, 2, 0, 0)),
    ((3, 1, 4, 0), (3, 1, 2, 0), (3, 2, 3, 0), (3, 2, 4, 0), (3, 2, 3, 0, 0), (3, 4, 3, 0, 1), (3, 4, 5, 0, 1), (3, 4, 2, 0, 0)),
    ((3, 2, 4, 0), (3, 1, 3, 0), (3, 2, 4, 0), (3, 2, 4, 0), (3, 3, 3, 0, 0), (3, 4, 3, 0, 1), (3, 4, 5, 1, 1), (3, 4, 3, 0, 0)),
    ((4, 2, 4, 0), (4, 1, 5, 0), (3, 3, 5, 0), (4, 2, 5, 0), (4, 4, 3, 0, 0), (4, 4, 3, 0, 1), (4, 4, 5, 2, 1), (4, 4, 3, 0, 0)),
    ((4, 3, 4, 0), (4, 1, 5, 0), (4, 3, 5, 0), (4, 2, 6, 0), (4, 4, 4, 0, 0), (4, 4, 3, 0, 1), (4, 4, 5, 3, 1), (4, 4, 6, 1, 0)),
    ((4, 3, 4, 0), (4, 3, 5, 0), (4, 3, 6, 0), (4, 3, 6, 0), (4, 4, 5, 0, 0), (4, 4, 3, 0, 3), (4, 4, 5, 3, 2), (4, 4, 7, 2, 2)),
    ((4, 4, 6, 0), (4, 3, 6, 0), (4, 3, 7, 0), (4, 4, 7, 0), (4, 4, 5, 1, 2), (4, 4, 5, 1, 3), (4, 4, 5, 4, 4), (4, 4, 7, 2, 2)),
    ((4, 4, 6, 0), (4, 3, 8, 0), (4, 4, 8, 0), (4, 4, 8, 0), (4, 4, 5, 4, 5), (4, 4, 5, 4, 5), (4, 4, 6, 5, 4), (4, 4, 7, 6, 3)),
    ((4, 4, 7, 4), (4, 3, 8, 0), (4, 4, 9, 1), (4, 4, 8, 0), (4, 4, 5, 4, 5), (4, 4, 6, 5, 5), (4, 4, 6, 6, 4), (4, 4, 7, 6, 3)),
    ((4, 4, 7, 4), (4, 3, 9, 4), (4, 4, 11, 4), (4, 4, 11, 2), (4, 4, 7, 8, 7), (4, 4, 7, 5, 8), (4, 4, 7, 8, 6), (4, 4, 7, 7, 4)),
    ((4, 4, 7, 6), (4, 3, 10, 4), (4, 4, 12, 5), (4, 4, 12, 4), (4, 4, 7, 8, 7), (4, 4, 7, 5, 8), (4, 4, 7, 8, 6), (4, 4, 7, 9, 4)),
    ((4, 4, 13, 8), (4, 3, 11, 4), (4, 4, 12, 5), (4, 4, 12, 4), (4, 4, 8, 8, 10), (4, 4, 8, 8, 11), (4, 4, 7, 9, 6), (4, 4, 8, 9, 6)),
    ((4, 4, 13, 8), (4, 4, 11, 8), (4, 4, 15, 5), (4, 4, 15, 6), (4, 4, 8, 9, 11), (4, 4, 8, 9, 11), (4, 4, 8, 11, 8), (4, 4, 8, 10, 6)),
    ((4, 4, 13, 8), (4, 4, 12, 8), (4, 4, 15, 6), (4, 4, 16, 6), (4, 4, 8, 11, 11), (4, 4, 8, 9, 12), (4, 4, 8, 11, 11), (4, 4, 8, 10, 8)),
    ((4, 4, 13, 8), (4, 4, 15, 8), (4, 4, 15, 6), (4, 4, 16, 6), (4, 4, 8, 11, 11), (4, 4, 8, 11, 13), (4, 4, 8, 11, 11), (4, 4, 8, 11, 10)),
    ((4, 4, 14, 8), (4, 4, 15, 8), (4, 4, 15, 7), (4, 4, 16, 10), (4, 4, 8, 12, 12), (4, 4, 8, 11, 14), (4, 4, 8, 13, 11), (4, 4, 8, 13, 12)),
    ((4, 4, 16, 8), (4, 4, 15, 8), (4, 4, 16, 7), (4, 4, 16, 10), (4, 4, 8, 12, 13), (4, 4, 8, 12, 14), (4, 4, 8, 14, 11), (4, 4, 8, 13, 12)),
    ((4, 4, 16, 9), (4, 4, 16, 10), (4, 4, 16, 9), (4, 4, 16, 12), (4, 4, 8, 13, 14), (4, 4, 8, 13, 14), (4, 4, 8, 15, 14), (4, 4, 8, 13, 13)),
    ((4, 4, 16, 10), (4, 4, 16, 12), (4, 4, 16, 12), (4, 4, 16, 12), (4, 4, 8, 13, 14), (4, 4, 8, 13, 15), (4, 4, 8, 15, 14), (4, 4, 8, 14, 13)),
    ((4, 4, 16, 10), (4, 4, 16, 12), (4, 4, 16, 13), (4, 4, 16, 12), (4, 4, 8, 13, 14), (4, 4, 8, 15, 15), (4, 4, 8, 15, 14), (4, 4, 8, 16, 13)),
    ((4, 4, 16, 10), (4, 4, 16, 12), (4, 4, 16, 13), (4, 4, 16, 16), (4, 4, 8, 15, 14), (4, 4, 8, 15, 16), (4, 4, 8, 16, 14), (4, 4, 8, 16, 16)),
    ((4, 4, 16, 13), (4, 4, 16, 12), (4, 4, 16, 14), (4, 4, 16, 16), (4, 4, 8, 15, 16), (4, 4, 8, 15, 16), (4, 4, 8, 16, 16), (4, 4, 8, 16, 16)),
    ((4, 4, 16, 13), (4, 4, 16, 12), (4, 4, 16, 14), (4, 4, 16, 16), (4, 4, 8, 16, 16), (4, 4, 8, 16, 16), (4, 4, 8, 16, 16), (4, 4, 8, 16, 16)),
    ((4, 4, 16, 14), (4, 4, 16, 12), (4, 4, 16, 14), (4, 4, 16, 16), (4, 4, 8, 16, 16), (4, 4, 8, 16, 16), (4, 4, 8, 16, 16), (4, 4, 8, 16, 16)),
    ((4, 4, 16, 15), (4, 4, 16, 16), (4, 4, 16, 16), (4, 4, 16, 16), (4, 4, 8, 16, 16), (4, 4, 8, 16, 16), (4, 4, 8, 16, 16), (4, 4, 8, 16, 16)),
    ((4, 4, 16, 16), (4, 4, 16, 16), (4, 4, 16, 16), (4, 4, 16, 16), (4, 4, 8, 16, 16), (4, 4, 8, 16, 16), (4, 4, 8, 16, 16), (4, 4, 8, 16, 16)),
    ((4, 4, 16, 16), (4, 4, 16, 16), (4, 4, 16, 16), (4, 4, 16, 16), (4, 4, 8, 16, 16), (4, 4, 8, 16, 16), (4, 4, 8, 16, 16), (4, 4, 8, 16, 16)),
    ((4, 4, 16, 16), (4, 4, 16, 16), (4, 4, 16, 16), (4, 4, 16, 16), (4, 4, 8, 16, 16), (4, 4, 8, 16, 16), (4, 4, 8, 16, 16), (4, 4, 8, 16, 16)),
)
PHASES = (
    (
        ((1, 0, 2), 1, (7, 3, 11)),
        ((0, 1), 1, (3, 7)),
        ((9, 10), 1, (39, 43)),
        ((10, 9, 8), 1, (43, 39, 35)),
        ((0, 9, 8), 1, (3, 39, 35)),
        ((0, 8), 1, (3, 35)),
        ((0, 1, 9, 8), 1, (3, 7, 39, 35)),
        ((9, 8), 1, (39, 35)),
    ),
    (
        ((8,), 0, (35,)),
        ((), 0, ()),
        ((8,), 0, (35,)),
        ((11,), 0, (47,)),
        ((1,), 0, (7,)),
        ((1,), 0, (7,)),
        ((), 0, ()),
        ((0,), 0, (3,)),
    ),
    (
        ((), 1, (6, 2)),
        ((9, 8), 0, (39, 35)),
        ((0, 1), 1, (3, 34, 6, 38)),
        ((0, 12), 0, (3, 51)),
        ((2, 10), 1, (34, 11, 42, 6)),
        ((10, 9), 1, (43, 2, 38)),
        ((10,), 0, (43,)),
        ((10, 1), 1, (42, 2, 6)),
    ),
    (
        ((10, 9), 0, (10, 43, 38)),
        ((2,), 1, (2, 6, 10, 38)),
        ((12, 13, 11), 0, (51, 55, 46, 47)),
        ((1, 13), 1, (7, 38, 42, 55, 34)),
        ((), 0, (2, 38, 43)),
        ((11,), 0, (47, 6, 34, 46, 42)),
        ((), 1, (6, 42, 34)),
        ((11,), 0, (47, 38, 34, 46)),
    ),
    (
        ((3,), 0, (15, 14, 42)),
        ((5,), 0, (11, 34, 23)),
        ((), 0, (7, 50, 2)),
        ((), 0, (54, 50, 6, 2, 46)),
        ((11,), 0, (46, 10, 47)),
        ((2,), 0, (39, 10, 11)),
        ((2, 11), 0, (2, 38, 10, 46)),
        ((2,), 0, (11, 10, 7)),
    ),
    (
        ((), 0, ()),
        ((11, 10), 0, (47, 43, 22)),
        ((14,), 0, (59,)),
        ((2, 14), 1, (9, 59, 58, 5)),
        ((12,), 0, (50, 51)),
        ((12,), 0, (51, 50)),
        ((12,), 0, (51, 50, 47, 11)),
        ((12,), 0, (51, 50)),
    ),
    (
        ((4, 5), 0, (18, 22, 39)),
        ((4,), 0, (18, 46, 19, 42)),
        ((2,), 0, (11, 54)),
        ((), 0, (45, 37, 41, 10, 33)),
        ((3,), 0, (15,)),
        ((13,), 1, (55, 41, 1, 37, 5)),
        ((3,), 1, (15, 33, 1, 13)),
        ((), 1, (37, 1, 41, 33)),
    ),
    (
        ((11,), 0, (46, 34, 19)),
        ((3,), 0, (15, 14)),
        ((), 1, (58, 10, 37)),
        ((15,), 0, (1, 11, 63)),
        ((), 1, (37, 1, 5)),
        ((3,), 0, (33, 15)),
        ((), 0, (5, 14, 41)),
        ((), 0, (5, 9, 45)),
    ),
    (
        ((), 1, (33, 9, 23, 5, 45)),
        ((6,), 1, (33, 41, 9, 25, 1)),
        ((), 0, (33, 45, 1)),
        ((3,), 0, (14, 15, 53, 62, 57)),
        ((4,), 0, (9, 41, 17, 45)),
        ((), 0, (54,)),
        ((13,), 0, (55,)),
        ((5, 3, 13), 0, (23, 15, 54)),
    ),
    (
        ((), 0, (13,)),
        ((), 0, (37, 27, 5, 21, 17)),
        ((15,), 0, (5, 41, 63)),
        ((), 1, (32, 49, 40, 0)),
        ((13,), 0, (14, 18, 55, 13)),
        ((), 0, (14, 13)),
        ((), 0, (45, 37, 9)),
        ((), 1, (13, 14, 4, 44, 43)),
    ),
    (
        ((6,), 0, (1, 47, 27, 26, 41)),
        ((7,), 0, (45, 31, 13)),
        ((3,), 1, (4, 42, 15, 57)),
        ((4,), 0, (36, 16)),
        ((), 0, (53, 49)),
        ((4,), 1, (16, 8, 19, 4, 17)),
        ((6,), 1, (8, 25, 32)),
        ((), 0, (49,)),
    ),
    (
        ((7,), 1, (0, 37, 30)),
        ((12,), 1, (4, 50)),
        ((5,), 0, (13, 36, 23)),
        ((), 0, (13, 44, 4, 18)),
        ((), 1, (44, 36, 19, 33, 32)),
        ((), 0, (9, 45, 49)),
        ((), 0, (4, 54)),
        ((), 0, (55, 40, 21)),
    ),
    (
        ((), 0, (21, 32, 31)),
        ((), 0, (0, 40, 20)),
        ((), 0, (9, 0, 21)),
        ((), 0, (61, 12, 48, 8)),
        ((), 0, (8, 12)),
        ((6,), 0, (27, 0, 40)),
        ((4,), 0, (18, 44, 53, 12, 19)),
        ((14,), 0, (57, 22, 32, 0)),
    ),
    (
        ((), 0, (44, 8, 4)),
        ((13,), 0, (24, 54, 36)),
        ((4,), 0, (17, 53, 8, 14)),
        ((6, 5), 0, (25, 52, 20)),
        ((6, 5), 0, (24, 16, 4, 23)),
        ((15, 5), 0, (63, 21)),
        ((5, 14), 0, (23, 59, 0, 22)),
        ((15, 7), 0, (8, 61, 30, 58)),
    ),
    (
        ((12,), 0, (51,)),
        ((), 0, (26, 49)),
        ((6,), 0, (20, 26, 12, 52)),
        ((), 0, (24, 27, 56)),
        ((14, 15), 0, (57, 61, 25, 21, 0)),
        ((14,), 0, (61, 32, 59)),
        ((15, 7), 0, (57, 61, 30, 17, 58)),
        ((), 0, (62,)),
    ),
    (
        ((13,), 0, (50, 55, 17, 49)),
        ((), 0, (30, 12, 8, 55)),
        ((), 0, (22, 16, 25, 49, 24)),
        ((), 0, (19,)),
        ((7,), 0, (20, 62, 58, 48, 28)),
        ((), 0, (36, 62, 23)),
        ((), 0, (31, 56, 29, 49)),
        ((6,), 0, (31, 29, 59, 24, 20)),
    ),
    (
        ((14,), 0, (12, 59, 54)),
        ((), 0, (16, 32, 53, 44)),
        ((), 0, (32, 62, 19)),
        ((), 0, (26,)),
        ((), 0, (54,)),
        ((7,), 0, (12, 30, 57)),
        ((), 0, (20, 62, 16, 27)),
        ((4,), 0, (17, 12, 25, 52)),
    ),
    (
        ((), 0, (36, 53, 57)),
        ((15, 14), 0, (28, 62, 59, 57, 51)),
        ((7,), 0, (61, 18, 40, 28)),
        ((7,), 0, (28, 29, 17)),
        ((), 0, (59, 56, 30)),
        ((), 0, (18, 48, 58, 52, 24)),
        ((), 0, (48, 26, 40)),
        ((), 0, (16, 28)),
    ),
    (
        ((15,), 0, (40, 20, 24, 25, 63)),
        ((), 0, (58, 48, 56, 63, 52)),
        ((), 0, (31, 48)),
        ((), 0, (22,)),
        ((), 0, (27, 52, 26)),
        ((), 0, (56, 31, 20, 44)),
        ((), 0, (52, 21, 36)),
        ((), 0, (36, 18, 53)),
    ),
    (
        ((), 0, (29, 48, 61, 58, 62)),
        ((), 0, (29,)),
        ((), 0, (44, 27)),
        ((), 0, (21,)),
        ((), 0, (22,)),
        ((), 0, (28, 53, 26, 60, 25)),
        ((), 0, ()),
        ((), 0, (26, 27, 63)),
    ),
    (
        ((), 0, (28, 52, 16, 56, 60)),
        ((), 0, (61, 60)),
        ((), 0, (29, 60, 30, 56)),
        ((), 0, (23, 30, 60, 31)),
        ((), 0, (40, 63, 29, 60, 31)),
        ((), 0, (22, 29)),
        ((), 0, (63, 60, 28, 24)),
        ((), 0, (48, 56, 60, 19)),
    ),
)


def quarter(dy, i):
    odd = dy % 2
    return (1 - odd) * (2 * (i % 2) + i // 2) + odd * ((i + 3 - dy) % 4)


def kernel(
    feats, starts, sw, taps, bias, w_ref, out_ref,
    rtaps, passing, fbuf, ext, gbuf, toep, xs, conv, mix, wts, part, got1, got2, done,
    f_sem, halo_ss, halo_rs, pass_rs, pass_ss, zx_ss, w_rs, sib_ss, zp_ss, zm_ss, x_ss, mix_ss, mix_rs,
    p_ss, got1_rs, got2_rs, out_sem,
):
    c, t = lax.axis_index("ctx"), lax.axis_index("tp")
    xh, z, k = c // 8, (c // 2) % 4, c % 2
    y, xl = t // 2, t % 2
    role = (xl + z) % 2

    def dev(xh, z, k, y, xl):
        return ((xh * 4 + z) * 2 + k, y * 2 + xl)

    sib = dev(xh, z, 1 - k, y, xl)
    zp, zm = dev(xh, (z + 1) % 4, k, y, xl), dev(xh, (z + 3) % 4, k, y, xl)
    yp, ym = dev(xh, z, k, (y + 1) % 4, xl), dev(xh, z, k, (y + 3) % 4, xl)
    xp, xn = dev(xh, z, k, y, 1 - xl), dev(1 - xh, z, k, y, 1 - xl)
    nxt, prv = ((c + 1) % 16, t), ((c + 15) % 16, t)

    f_copies = []
    for s in range(3):
        cp = pltpu.make_async_copy(feats.at[s], fbuf.at[s, pl.ds(HALO, ROWS)], f_sem.at[s])
        cp.start()
        f_copies.append(cp)

    barrier = pltpu.get_barrier_semaphore()
    for d in (sib, zp, zm, yp, ym, xp, xn, prv):
        pl.semaphore_signal(barrier, inc=1, device_id=d, device_id_type=MESH)
    pl.semaphore_wait(barrier, 8)

    def remote(src, dst, ss, rs, d):
        return pltpu.make_async_remote_copy(
            src_ref=src, dst_ref=dst, send_sem=ss, recv_sem=rs, device_id=d, device_id_type=MESH
        )

    dy_own = (2 * xh + z // 2 - y + 4) % 4

    def w_piece(h):
        return w_ref.at[:, pl.ds(h * LANES, LANES)]

    def slot(dy, h, r, core):
        return wts.at[dy, h, r, :, pl.ds(pl.multiple_of(core * LANES, LANES), LANES)]

    def x_copy(i, side):
        h = quarter(dy_own, i)
        return remote(
            w_piece(h), slot(dy_own, h, 1, k), x_ss.at[i, side], w_rs.at[dy_own, h, 1, k], (xp, xn)[side]
        )

    def pass_copy(i):
        h = quarter(dy_own, i)
        return remote(w_piece(h), passing.at[i], x_ss.at[i, 0], pass_rs.at[i], xp)

    def z_pass_copy(i, side):
        h = quarter(dy_own, i)
        return remote(
            w_piece(h), passing.at[4 * side + i], zx_ss.at[i, side], pass_rs.at[4 * side + i], (zp, zm)[side]
        )

    def z_onward_copy(i, side):
        dy = (2 * xh + ((z + 3 + 2 * side) % 4) // 2 - y + 4) % 4
        h = quarter(dy, i)
        return remote(
            passing.at[4 * side + i], slot(dy, h, 1, k), pass_ss.at[4 * side + i], w_rs.at[dy, h, 1, k], xn
        )

    def onward_copy(i):
        h = quarter(dy_own, i)
        return remote(passing.at[i], slot(dy_own, h, 0, k), pass_ss.at[i], w_rs.at[dy_own, h, 0, k], xn)

    halo_f = remote(
        feats.at[:, pl.ds(ROWS - HALO, HALO)], fbuf.at[:, pl.ds(0, HALO)], halo_ss.at[0], halo_rs.at[0], nxt
    )
    halo_f.start()

    @pl.when(role == 0)
    def _():
        for i in range(4):
            h = quarter(dy_own, i)
            pltpu.make_async_copy(w_piece(h), slot(dy_own, h, 0, k), w_rs.at[dy_own, h, 0, k]).start()

    def sib_copy(dy, h, r):
        here = slot(dy, h, r, k)
        return remote(here, here, sib_ss.at[dy, h, r], w_rs.at[dy, h, r, k], sib)

    def zp_copy(dy, h, r):
        here = slot(dy, h, r, k)
        return remote(here, here, zp_ss.at[dy, h, r], w_rs.at[dy, h, r, k], zp)

    def zm_copy(dy, h, r):
        here = slot(dy, h, r, k)
        return remote(here, here, zm_ss.at[dy, h, r], w_rs.at[dy, h, r, k], zm)

    def w_wait(dy, h, r, core):
        here = slot(dy, h, r, core)
        remote(here, here, sib_ss.at[dy, h, r], w_rs.at[dy, h, r, core], sib).wait_recv()

    kind_here = (z // 2 + y) % 2
    kind_below = (((z + 3) % 4) // 2 + y) % 2
    first_odd = 1 + 2 * ((((y + 1) % 4) // 2 + xh) % 2)

    def unit_of(kind, u):
        dy0, i0 = 2 - 2 * (u // 4), u % 4
        odd = u % 2
        dy1, i1 = first_odd * (1 - odd) + (4 - first_odd) * odd, u // 2
        dy, i = dy0 + kind * (dy1 - dy0), i0 + kind * (i1 - i0)
        return dy, quarter(dy, i)

    def side_of(dy):
        return (((y + dy) % 4) // 2 + xh) % 2

    def piece_of(kind, n):
        dy, h = unit_of(kind, n // 2)
        return dy, h, (n + side_of(dy)) % 2

    far_side = side_of(2)
    kind = kind_here + role * (kind_below - kind_here)
    cls = role * 4 + kind * 2 + far_side

    def pick(values):
        a, b, c2, d = values
        if a == b == c2 == d:
            return a
        return a + far_side * (b - a) + kind * (c2 - a) + kind * far_side * (d - c2 - b + a)

    def pick_any(values):
        if all(v == values[0] for v in values):
            return values[0]
        picked = jnp.int32(values[0])
        for n in range(1, 8):
            picked = jnp.where(cls == n, jnp.int32(values[n]), picked)
        return picked

    def xp_step(n):
        @pl.when(role == 0)
        def _():
            pass_copy(n).start()

        @pl.when(role == 1)
        def _():
            x_copy(n, 0).start()

    def z_pass_step(n):
        z_pass_copy(n, 0).start()
        z_pass_copy(n, 1).start()

    def z_onward_step(n):
        for side in range(2):
            z_pass_copy(n, side).wait_recv()
            z_onward_copy(n, side).start()

    def at(which, base, n):
        code = jnp.int32(0)
        for m in range(16):
            code = jnp.where(n == m, pick([ORDERS[base + q][which][m] for q in range(4)]), code)
        return code

    def spread_step(n):
        code = at(0, 0, n)
        t, i = code // 4, code % 4
        dy = (dy_own + 2 * (t // 2)) % 4
        h, r = quarter(dy, i), t % 2
        w_wait(dy, h, r, k)

        @pl.when(t != 3)
        def _():
            zp_copy(dy, h, r).start()
            zm_copy(dy, h, r).start()

        sib_copy(dy, h, r).start()

    def relay_step(n):
        dy, h, r = piece_of(1 - kind_here, at(1, 0, n))
        w_wait(dy, h, r, k)
        sib_copy(dy, h, r).start()

    def xn_step(n):
        i = n // 2

        @pl.when(n % 2 == 0)
        def _():
            x_copy(i, 1).start()

        @pl.when(n % 2 == 1)
        def _():
            pass_copy(i).wait_recv()
            onward_copy(i).start()

    def from_below_step(n):
        dy, h, r = piece_of(kind_below, at(0, 4, n))
        w_wait(dy, h, r, k)

        @pl.when(r == 0)
        def _():
            zp_copy(dy, h, r).start()

        sib_copy(dy, h, r).start()

    def from_above_step(n):
        dy, h, r = piece_of(1 - kind_below, at(1, 4, n))
        w_wait(dy, h, r, k)

        @pl.when(r == 1)
        def _():
            zm_copy(dy, h, r).start()

        sib_copy(dy, h, r).start()

    sequences = (
        (xp_step, z_onward_step, spread_step, relay_step),
        (xp_step, z_pass_step, xn_step, from_below_step, from_above_step),
    )

    def transfers(point):
        for r in range(2):
            now = TRANSFERS[point][4 * r : 4 * r + 4]
            then = TRANSFERS[point - 1][4 * r : 4 * r + 4] if point else ((0,) * 5,) * 4
            if now == then:
                continue

            @pl.when(role == r)
            def _():
                for q, step in enumerate(sequences[r]):
                    lo, hi = [v[q] for v in then], [v[q] for v in now]
                    if lo != hi:
                        def body(n, _, step=step):
                            step(n)
                            return 0

                        lax.fori_loop(pick(lo), pick(hi), body, 0)

    ends = lax.broadcasted_iota(jnp.int32, (BLK, BLK), 0) + lax.broadcasted_iota(jnp.int32, (BLK, BLK), 1)
    mirror = (ends == BLK - 1).astype(F32).astype(BF16)
    rtaps[:, pl.ds(0, BLK)] = jnp.dot(taps[...].astype(BF16), mirror, preferred_element_type=F32)
    rtaps[:, pl.ds(BLK, BLK)] = jnp.zeros((CH // GROUP, BLK), F32)

    def toep_body(g, _):
        row = jnp.broadcast_to(rtaps[pl.ds(g, 1)], (BLK, 2 * BLK))
        toep[g] = pltpu.roll(row, 1, 1, stride=1, stride_axis=0).astype(BF16)
        return 0

    transfers(0)
    lax.fori_loop(0, CH // GROUP // 2, toep_body, 0)
    transfers(1)
    lax.fori_loop(CH // GROUP // 2, CH // GROUP, toep_body, 0)
    transfers(2)

    first = (c > 0).astype(F32)

    def keep_of(b):
        kept = (1 - starts[b]).astype(F32)
        return kept * jnp.where(b == 0, first, 1.0)

    def short(s, b, keep, lanes):
        tail = fbuf[s, pl.ds(pl.multiple_of(b * BLK, BLK), HALO), lanes].astype(F32)
        ext[s, pl.ds(0, 8), lanes] = tail[8:] * keep
        ext[s, pl.ds(8, BLK), lanes] = fbuf[
            s, pl.ds(pl.multiple_of(b * BLK + HALO, HALO), BLK), lanes
        ].astype(F32)
        total = sw[s, pl.ds(0, 1), lanes] * ext[s, pl.ds(8, BLK), lanes]
        for j in range(1, SPAN):
            total += sw[s, pl.ds(j, 1), lanes] * ext[s, pl.ds(8 - j, BLK), lanes]
        return total

    def lanes_of(lt):
        return pl.ds(pl.multiple_of(lt * LANES, LANES), LANES)

    def gate(b):
        keep = keep_of(b)

        def body(lt, _):
            lanes = lanes_of(lt)
            gbuf[b + 1, :, lanes] = (short(1, b, keep, lanes) * short(2, b, keep, lanes)).astype(BF16)
            return 0

        lax.fori_loop(0, CH // LANES, body, 0)

    def mix_copy(m):
        rows = pl.ds(m * CHUNK, CHUNK)
        return remote(mix.at[0, rows], mix.at[1, rows], mix_ss.at[m], mix_rs.at[m], xp)

    lane_group = lax.broadcasted_iota(jnp.int32, (BLK, 2 * LANES), 1) % LANES // GROUP

    def mix_pair(b0, lo, hi):
        keeps = [keep_of(b0), keep_of(b0 + 1)]

        def body(lt, _):
            lanes = lanes_of(lt)
            for i in range(2):
                cols = pl.ds(i * LANES, LANES)
                xs[pl.ds(0, BLK), cols] = (gbuf[b0 + i, :, lanes].astype(F32) * keeps[i]).astype(BF16)
                xs[pl.ds(BLK, BLK), cols] = gbuf[b0 + i + 1, :, lanes]
            mats = toep[pl.ds(lt * PER_TILE, PER_TILE)].reshape(PER_TILE * BLK, 2 * BLK)
            every = jnp.dot(mats, xs[...], preferred_element_type=F32)
            every = every.reshape(PER_TILE, BLK, 2 * LANES)
            picked = every[0]
            for g in range(1, PER_TILE):
                picked = jnp.where(lane_group == g, every[g], picked)
            conv[...] = picked
            for i in range(2):
                gated = gbuf[b0 + i + 1, :, lanes].astype(F32)
                query = short(0, b0 + i, keeps[i], lanes)
                direct = conv[:, pl.ds(i * LANES, LANES)] + bias[:, lanes] * gated
                mix[0, pl.ds(pl.multiple_of((b0 + i) * BLK, BLK), BLK), lanes] = (query * direct).astype(BF16)
            return 0

        lax.fori_loop(lo, hi, body, 0)

    chunk_at = [NCHUNK - 1 - i for i in range(NCHUNK)]

    tiles = CH // LANES
    for cp in f_copies:
        cp.wait()
    gate(NB - 1)
    halo_g = remote(gbuf.at[NB], gbuf.at[0], halo_ss.at[1], halo_rs.at[1], nxt)
    halo_g.start()
    transfers(3)
    point = 4
    for m in chunk_at:
        if m > 0:
            gate(2 * m)
            gate(2 * m - 1)
        else:
            halo_f.wait_recv()
            gate(0)
            halo_g.wait_recv()
        transfers(point)
        point += 1
        if m == NCHUNK - 1:
            mix_pair(2 * m, 0, tiles // 2)
            transfers(point)
            point += 1
            mix_pair(2 * m, tiles // 2, tiles)
        else:
            mix_pair(2 * m, 0, tiles)
        mix_copy(m).start()
        transfers(point)
        point += 1

    def rows_of(m):
        return pl.ds(pl.multiple_of(m * CHUNK, CHUNK), CHUNK)

    def project(dy, h, m):
        rows = rows_of(m)
        total = jnp.dot(mix[0, rows], wts[dy, h, 0], preferred_element_type=F32)
        return total + jnp.dot(mix[1, rows], wts[dy, h, 1], preferred_element_type=F32)

    def to_y(dy):
        return dev(xh, z, k, (y + dy) % 4, xl)

    def far_copy(v, m):
        dy, h = 2, quarter(2, v)
        here = part.at[dy, h, rows_of(m)]
        return remote(here, got1.at[h, rows_of(m)], p_ss.at[dy, h, m], got1_rs.at[h, m], to_y(1 + 2 * (v % 2)))

    def near_copy(u, m):
        dy, h = unit_of(1, u)
        here = part.at[dy, h, rows_of(m)]
        there = got2.at[dy // 2, h, rows_of(m)]
        return remote(here, there, p_ss.at[dy, h, m], got2_rs.at[dy // 2, h, m], to_y(dy))

    def got1_wait(h, m):
        there = got1.at[h, rows_of(m)]
        remote(there, there, p_ss.at[0, h, m], got1_rs.at[h, m], yp).wait_recv()

    def got2_wait(side, h, m):
        there = got2.at[side, h, rows_of(m)]
        remote(there, there, p_ss.at[0, h, m], got2_rs.at[side, h, m], yp).wait_recv()

    def tile_step(_, packed):
        code = packed % 64
        knd, u, m = code // 32, code // 4 % 8, code % 4
        dy, h = unit_of(knd, u)
        rows = rows_of(m)
        total = project(dy, h, m)
        depends = (knd == 1) & (u >= 4)

        @pl.when(depends)
        def _():
            got1_wait(h, m)
            part[dy, h, rows] = (total + got1[h, rows].astype(F32)).astype(BF16)

        @pl.when(jnp.logical_not(depends))
        def _():
            part[dy, h, rows] = total.astype(BF16)

        @pl.when((knd == 0) & (u < 4))
        def _():
            far_copy(u, m).start()

        @pl.when(knd == 1)
        def _():
            near_copy(u, m).start()

        return packed // 64

    chunks = [0] * 8
    for p, phase in enumerate(PHASES):
        if p:
            transfers(point)
            point += 1
        for n, (waits, _, _) in enumerate(phase):
            if waits:
                @pl.when(cls == n)
                def _():
                    for code in waits:
                        dy, h = unit_of(code // 8, code % 8)
                        for r in range(2):
                            w_wait(dy, h, r, 1 - k)

        before = list(chunks)
        chunks = [a + row[1] for a, row in zip(chunks, phase)]
        if before != chunks:
            def chunk_step(n, _):
                mix_copy(NCHUNK - 1 - n).wait_recv()
                return 0

            lax.fori_loop(pick_any(before), pick_any(chunks), chunk_step, 0)
        packed = [sum(code * 64**n for n, code in enumerate(row[2])) for row in phase]
        lax.fori_loop(0, pick_any([len(row[2]) for row in phase]), tile_step, pick_any(packed) + jnp.int32(0))

    halo_f.wait_send()
    halo_g.wait_send()
    for m in range(NCHUNK):
        mix_copy(m).wait_send()

    def sent_body(u, _):
        for knd in range(2):
            dy, h = unit_of(knd, u)
            for r in range(2):
                sib_copy(dy, h, r).wait_send()

        @pl.when(role == 1)
        def _():
            dya, ha = unit_of(kind_below, u)
            dyb, hb = unit_of(1 - kind_below, u)
            zp_copy(dya, ha, 0).wait_send()
            zm_copy(dyb, hb, 1).wait_send()

        return 0

    lax.fori_loop(0, 8, sent_body, 0)

    def early_sent_body(v, _):
        for m in range(NCHUNK):
            far_copy(v, m).wait_send()
            near_copy(v, m).wait_send()

        @pl.when(role == 0)
        def _():
            pass_copy(v).wait_send()
            for t in range(3):
                dy = (dy_own + 2 * (t // 2)) % 4
                zp_copy(dy, quarter(dy, v), t % 2).wait_send()
                zm_copy(dy, quarter(dy, v), t % 2).wait_send()
            z_onward_copy(v, 0).wait_send()
            z_onward_copy(v, 1).wait_send()

        @pl.when(role == 1)
        def _():
            x_copy(v, 0).wait_send()
            x_copy(v, 1).wait_send()
            onward_copy(v).wait_send()
            z_pass_copy(v, 0).wait_send()
            z_pass_copy(v, 1).wait_send()

        return 0

    lax.fori_loop(0, 4, early_sent_body, 0)

    def out_copy(h, m):
        rows = rows_of(m)
        for core in range(2):
            yield pltpu.make_async_copy(
                done.at[h, rows, pl.ds(core * LANES, LANES)],
                out_ref.at[rows, pl.ds(pl.multiple_of(core * 512 + h * LANES, LANES), LANES)],
                out_sem.at[h, m, core],
            )

    def sum_body(n, _):
        i, m = n // NCHUNK, NCHUNK - 1 - n % NCHUNK
        h = 2 * (i % 2) + i // 2
        rows = rows_of(m)
        got2_wait(0, h, m)
        got2_wait(1, h, m)
        total = part[0, h, rows].astype(F32) + got2[0, h, rows].astype(F32) + got2[1, h, rows].astype(F32)
        done[h, rows] = total.astype(done.dtype)
        for cp in out_copy(h, m):
            cp.start()
        return 0

    lax.fori_loop(0, 4 * NCHUNK, sum_body, 0)

    def late_sent_body(u, _):
        for m in range(NCHUNK):
            near_copy(u, m).wait_send()
            for cp in out_copy(u - 4, m):
                cp.wait()
        return 0

    lax.fori_loop(4, 8, late_sent_body, 0)


def on_device(features, contig_starts, short_filter, medium_filter, filter_bias, out_weight):
    vmem = pl.BlockSpec(memory_space=pltpu.VMEM)
    hbm = pl.BlockSpec(memory_space=pl.ANY)
    dma = pltpu.SemaphoreType.DMA
    return pl.pallas_call(
        kernel,
        out_shape=jax.ShapeDtypeStruct((ROWS, CH), OUT),
        in_specs=[hbm, pl.BlockSpec(memory_space=pltpu.SMEM), vmem, vmem, vmem, hbm],
        out_specs=hbm,
        scratch_shapes=[
            pltpu.VMEM((CH // GROUP, 2 * BLK), F32),
            pltpu.VMEM((8, CH, LANES), BF16),
            pltpu.VMEM((3, HALO + ROWS, CH), BF16),
            pltpu.VMEM((3, 8 + BLK, CH), F32),
            pltpu.VMEM((NB + 1, BLK, CH), BF16),
            pltpu.VMEM((CH // GROUP, BLK, 2 * BLK), BF16),
            pltpu.VMEM((2 * BLK, 2 * LANES), BF16),
            pltpu.VMEM((BLK, 2 * LANES), F32),
            pltpu.VMEM((2, ROWS, CH), BF16),
            pltpu.VMEM((4, 4, 2, CH, 2 * LANES), BF16),
            pltpu.VMEM((4, 4, ROWS, 2 * LANES), BF16),
            pltpu.VMEM((4, ROWS, 2 * LANES), BF16),
            pltpu.VMEM((2, 4, ROWS, 2 * LANES), BF16),
            pltpu.VMEM((4, ROWS, 2 * LANES), OUT),
            dma((3,)),
            dma((2,)),
            dma((2,)),
            dma((8,)),
            dma((8,)),
            dma((4, 2)),
            dma((4, 4, 2, 2)),
            dma((4, 4, 2)),
            dma((4, 4, 2)),
            dma((4, 4, 2)),
            dma((4, 2)),
            dma((NCHUNK,)),
            dma((NCHUNK,)),
            dma((4, 4, NCHUNK)),
            dma((4, NCHUNK)),
            dma((2, 4, NCHUNK)),
            dma((4, NCHUNK, 2)),
        ],
        compiler_params=pltpu.CompilerParams(
            collective_id=0, has_side_effects=True, vmem_limit_bytes=60 * 1024 * 1024
        ),
        cost_estimate=pl.CostEstimate(
            flops=2 * ROWS * 2048 * 4096, bytes_accessed=16 * 1024 * 1024, transcendentals=0
        ),
    )(
        jnp.transpose(features, (1, 0, 2)),
        contig_starts,
        jnp.transpose(short_filter, (1, 0, 2)),
        medium_filter,
        filter_bias.reshape(1, CH),
        out_weight,
    )


def solution(mesh):
    in_specs = (
        P("ctx", None, "tp"),
        P("ctx"),
        P(None, None, "tp"),
        P("tp", None),
        P("tp"),
        P("tp", "ctx"),
    )
    out_specs = P("ctx", "tp")
    return jax.shard_map(
        on_device, mesh=mesh, in_specs=in_specs, out_specs=out_specs, check_vma=False
    )
```

```python
import jax
import jax.numpy as jnp
from jax import lax
from jax.experimental import pallas as pl
from jax.experimental.pallas import tpu as pltpu
from jax.sharding import PartitionSpec as P

MESH = pl.DeviceIdType.MESH
F32 = jnp.float32
BF16 = jnp.bfloat16

ROWS = 1024
CH = 1024
BLK = 128
NB = ROWS // BLK
SPAN = 7
HALO = 16
GROUP = 16
OUT = jnp.bfloat16
LANES = 128
PER_TILE = LANES // GROUP
CHUNK = 256
NCHUNK = ROWS // CHUNK


ORDERS = (
    ((0, 4, 1, 5, 6, 2, 3, 7, 8, 14, 13, 9, 12, 10, 15, 11), (3, 1, 0, 2, 4, 5, 7, 6, 9, 10, 11, 8, 13, 12, 15, 14)),
    ((0, 1, 12, 8, 4, 9, 5, 13, 14, 10, 2, 15, 11, 6, 3, 7), (0, 1, 3, 2, 4, 6, 5, 7, 10, 9, 8, 11, 14, 15, 12, 13)),
    ((0, 4, 5, 12, 8, 1, 13, 9, 2, 14, 6, 10, 7, 15, 3, 11), (2, 0, 3, 1, 4, 5, 10, 7, 6, 8, 9, 11, 12, 13, 15, 14)),
    ((0, 1, 4, 8, 13, 5, 12, 9, 2, 14, 6, 10, 15, 3, 7, 11), (1, 0, 2, 3, 4, 5, 6, 11, 8, 7, 12, 9, 15, 10, 14, 13)),
    ((0, 2, 1, 3, 5, 10, 8, 4, 12, 6, 7, 9, 11, 14, 13, 15), (2, 1, 3, 0, 5, 6, 4, 7, 8, 9, 10, 11, 13, 14, 15, 12)),
    ((0, 1, 9, 2, 3, 5, 4, 8, 6, 7, 10, 11, 12, 14, 13, 15), (0, 1, 2, 3, 5, 6, 7, 4, 9, 10, 8, 11, 14, 13, 15, 12)),
    ((0, 2, 1, 3, 5, 6, 4, 7, 10, 8, 9, 11, 14, 13, 12, 15), (0, 1, 2, 3, 4, 5, 6, 10, 7, 8, 12, 9, 13, 11, 14, 15)),
    ((0, 1, 3, 2, 4, 5, 7, 6, 8, 9, 11, 10, 12, 15, 13, 14), (1, 0, 2, 3, 4, 5, 10, 11, 6, 8, 7, 12, 9, 14, 15, 13)),
)
TRANSFERS = (
    ((1, 0, 0, 0), (1, 0, 0, 0), (2, 0, 1, 0), (2, 0, 0, 0), (1, 1, 1, 0, 0), (2, 1, 0, 0, 0), (1, 2, 1, 0, 0), (2, 1, 0, 0, 0)),
    ((2, 0, 1, 0), (1, 0, 0, 0), (2, 0, 1, 0), (3, 0, 1, 0), (1, 1, 1, 0, 0), (2, 1, 0, 0, 0), (1, 3, 1, 0, 0), (2, 2, 0, 0, 0)),
    ((2, 0, 1, 0), (2, 0, 0, 0), (3, 0, 1, 0), (3, 0, 1, 0), (3, 2, 1, 0, 0), (2, 2, 0, 0, 0), (3, 3, 1, 0, 0), (2, 2, 0, 0, 0)),
    ((2, 0, 1, 0), (3, 0, 1, 0), (3, 0, 1, 0), (3, 0, 2, 0), (3, 2, 1, 0, 0), (2, 2, 1, 0, 0), (3, 3, 3, 0, 0), (2, 2, 1, 0, 0)),
    ((2, 0, 2, 0), (3, 1, 2, 0), (3, 1, 2, 0), (3, 0, 3, 0), (3, 2, 1, 0, 0), (2, 4, 2, 0, 0), (3, 3, 3, 0, 0), (3, 3, 2, 0, 0)),
    ((2, 0, 3, 0), (3, 1, 2, 0), (3, 1, 3, 0), (3, 2, 4, 0), (3, 2, 3, 0, 0), (2, 4, 3, 0, 0), (3, 4, 3, 0, 0), (3, 4, 2, 0, 0)),
    ((3, 1, 4, 0), (3, 1, 2, 0), (3, 2, 3, 0), (3, 2, 4, 0), (3, 2, 3, 0, 0), (3, 4, 3, 0, 1), (3, 4, 5, 0, 1), (3, 4, 2, 0, 0)),
    ((3, 2, 4, 0), (3, 1, 3, 0), (3, 2, 4, 0), (3, 2, 4, 0), (3, 3, 3, 0, 0), (3, 4, 3, 0, 1), (3, 4, 5, 1, 1), (3, 4, 3, 0, 0)),
    ((4, 2, 4, 0), (4, 1, 5, 0), (3, 3, 5, 0), (4, 2, 5, 0), (4, 4, 3, 0, 0), (4, 4, 3, 0, 1), (4, 4, 5, 2, 1), (4, 4, 3, 0, 0)),
    ((4, 3, 4, 0), (4, 1, 5, 0), (4, 3, 5, 0), (4, 2, 6, 0), (4, 4, 4, 0, 0), (4, 4, 3, 0, 1), (4, 4, 5, 3, 1), (4, 4, 6, 1, 0)),
    ((4, 3, 4, 0), (4, 3, 5, 0), (4, 3, 6, 0), (4, 3, 6, 0), (4, 4, 5, 0, 0), (4, 4, 3, 0, 3), (4, 4, 5, 3, 2), (4, 4, 7, 2, 2)),
    ((4, 4, 6, 0), (4, 3, 6, 0), (4, 3, 7, 0), (4, 4, 7, 0), (4, 4, 5, 1, 2), (4, 4, 5, 1, 3), (4, 4, 5, 4, 4), (4, 4, 7, 2, 2)),
    ((4, 4, 6, 0), (4, 3, 8, 0), (4, 4, 8, 0), (4, 4, 8, 0), (4, 4, 5, 4, 5), (4, 4, 5, 4, 5), (4, 4, 6, 5, 4), (4, 4, 7, 6, 3)),
    ((4, 4, 7, 4), (4, 3, 8, 0), (4, 4, 9, 1), (4, 4, 8, 0), (4, 4, 5, 4, 5), (4, 4, 6, 5, 5), (4, 4, 6, 6, 4), (4, 4, 7, 6, 3)),
    ((4, 4, 7, 4), (4, 3, 9, 4), (4, 4, 11, 4), (4, 4, 11, 2), (4, 4, 7, 8, 7), (4, 4, 7, 5, 8), (4, 4, 7, 8, 6), (4, 4, 7, 7, 4)),
    ((4, 4, 7, 6), (4, 3, 10, 4), (4, 4, 12, 5), (4, 4, 12, 4), (4, 4, 7, 8, 7), (4, 4, 7, 5, 8), (4, 4, 7, 8, 6), (4, 4, 7, 9, 4)),
    ((4, 4, 13, 8), (4, 3, 11, 4), (4, 4, 12, 5), (4, 4, 12, 4), (4, 4, 8, 8, 10), (4, 4, 8, 8, 11), (4, 4, 7, 9, 6), (4, 4, 8, 9, 6)),
    ((4, 4, 13, 8), (4, 4, 11, 8), (4, 4, 15, 5), (4, 4, 15, 6), (4, 4, 8, 9, 11), (4, 4, 8, 9, 11), (4, 4, 8, 11, 8), (4, 4, 8, 10, 6)),
    ((4, 4, 13, 8), (4, 4, 12, 8), (4, 4, 15, 6), (4, 4, 16, 6), (4, 4, 8, 11, 11), (4, 4, 8, 9, 12), (4, 4, 8, 11, 11), (4, 4, 8, 10, 8)),
    ((4, 4, 13, 8), (4, 4, 15, 8), (4, 4, 15, 6), (4, 4, 16, 6), (4, 4, 8, 11, 11), (4, 4, 8, 11, 13), (4, 4, 8, 11, 11), (4, 4, 8, 11, 10)),
    ((4, 4, 14, 8), (4, 4, 15, 8), (4, 4, 15, 7), (4, 4, 16, 10), (4, 4, 8, 12, 12), (4, 4, 8, 11, 14), (4, 4, 8, 13, 11), (4, 4, 8, 13, 12)),
    ((4, 4, 16, 8), (4, 4, 15, 8), (4, 4, 16, 7), (4, 4, 16, 10), (4, 4, 8, 12, 13), (4, 4, 8, 12, 14), (4, 4, 8, 14, 11), (4, 4, 8, 13, 12)),
    ((4, 4, 16, 9), (4, 4, 16, 10), (4, 4, 16, 9), (4, 4, 16, 12), (4, 4, 8, 13, 14), (4, 4, 8, 13, 14), (4, 4, 8, 15, 14), (4, 4, 8, 13, 13)),
    ((4, 4, 16, 10), (4, 4, 16, 12), (4, 4, 16, 12), (4, 4, 16, 12), (4, 4, 8, 13, 14), (4, 4, 8, 13, 15), (4, 4, 8, 15, 14), (4, 4, 8, 14, 13)),
    ((4, 4, 16, 10), (4, 4, 16, 12), (4, 4, 16, 13), (4, 4, 16, 12), (4, 4, 8, 13, 14), (4, 4, 8, 15, 15), (4, 4, 8, 15, 14), (4, 4, 8, 16, 13)),
    ((4, 4, 16, 10), (4, 4, 16, 12), (4, 4, 16, 13), (4, 4, 16, 16), (4, 4, 8, 15, 14), (4, 4, 8, 15, 16), (4, 4, 8, 16, 14), (4, 4, 8, 16, 16)),
    ((4, 4, 16, 13), (4, 4, 16, 12), (4, 4, 16, 14), (4, 4, 16, 16), (4, 4, 8, 15, 16), (4, 4, 8, 15, 16), (4, 4, 8, 16, 16), (4, 4, 8, 16, 16)),
    ((4, 4, 16, 13), (4, 4, 16, 12), (4, 4, 16, 14), (4, 4, 16, 16), (4, 4, 8, 16, 16), (4, 4, 8, 16, 16), (4, 4, 8, 16, 16), (4, 4, 8, 16, 16)),
    ((4, 4, 16, 14), (4, 4, 16, 12), (4, 4, 16, 14), (4, 4, 16, 16), (4, 4, 8, 16, 16), (4, 4, 8, 16, 16), (4, 4, 8, 16, 16), (4, 4, 8, 16, 16)),
    ((4, 4, 16, 15), (4, 4, 16, 16), (4, 4, 16, 16), (4, 4, 16, 16), (4, 4, 8, 16, 16), (4, 4, 8, 16, 16), (4, 4, 8, 16, 16), (4, 4, 8, 16, 16)),
    ((4, 4, 16, 16), (4, 4, 16, 16), (4, 4, 16, 16), (4, 4, 16, 16), (4, 4, 8, 16, 16), (4, 4, 8, 16, 16), (4, 4, 8, 16, 16), (4, 4, 8, 16, 16)),
    ((4, 4, 16, 16), (4, 4, 16, 16), (4, 4, 16, 16), (4, 4, 16, 16), (4, 4, 8, 16, 16), (4, 4, 8, 16, 16), (4, 4, 8, 16, 16), (4, 4, 8, 16, 16)),
    ((4, 4, 16, 16), (4, 4, 16, 16), (4, 4, 16, 16), (4, 4, 16, 16), (4, 4, 8, 16, 16), (4, 4, 8, 16, 16), (4, 4, 8, 16, 16), (4, 4, 8, 16, 16)),
)
PHASES = (
    (
        ((1, 0, 2), 1, (7, 3, 11)),
        ((0, 1), 1, (3, 7)),
        ((9, 10), 1, (39, 43)),
        ((10, 9, 8), 1, (43, 39, 35)),
        ((0, 9, 8), 1, (3, 39, 35)),
        ((0, 8), 1, (3, 35)),
        ((0, 1, 9, 8), 1, (3, 7, 39, 35)),
        ((9, 8), 1, (39, 35)),
    ),
    (
        ((8,), 0, (35,)),
        ((), 0, ()),
        ((8,), 0, (35,)),
        ((11,), 0, (47,)),
        ((1,), 0, (7,)),
        ((1,), 0, (7,)),
        ((), 0, ()),
        ((0,), 0, (3,)),
    ),
    (
        ((), 1, (6, 2)),
        ((9, 8), 0, (39, 35)),
        ((0, 1), 1, (3, 34, 6, 38)),
        ((0, 12), 0, (3, 51)),
        ((2, 10), 1, (34, 11, 42, 6)),
        ((10, 9), 1, (43, 2, 38)),
        ((10,), 0, (43,)),
        ((10, 1), 1, (42, 2, 6)),
    ),
    (
        ((10, 9), 0, (10, 43, 38)),
        ((2,), 1, (2, 6, 10, 38)),
        ((12, 13, 11), 0, (51, 55, 46, 47)),
        ((1, 13), 1, (7, 38, 42, 55, 34)),
        ((), 0, (2, 38, 43)),
        ((11,), 0, (47, 6, 34, 46, 42)),
        ((), 1, (6, 42, 34)),
        ((11,), 0, (47, 38, 34, 46)),
    ),
    (
        ((3,), 0, (15, 14, 42)),
        ((5,), 0, (11, 34, 23)),
        ((), 0, (7, 50, 2)),
        ((), 0, (54, 50, 6, 2, 46)),
        ((11,), 0, (46, 10, 47)),
        ((2,), 0, (39, 10, 11)),
        ((2, 11), 0, (2, 38, 10, 46)),
        ((2,), 0, (11, 10, 7)),
    ),
    (
        ((), 0, ()),
        ((11, 10), 0, (47, 43, 22)),
        ((14,), 0, (59,)),
        ((2, 14), 1, (9, 59, 58, 5)),
        ((12,), 0, (50, 51)),
        ((12,), 0, (51, 50)),
        ((12,), 0, (51, 50, 47, 11)),
        ((12,), 0, (51, 50)),
    ),
    (
        ((4, 5), 0, (18, 22, 39)),
        ((4,), 0, (18, 46, 19, 42)),
        ((2,), 0, (11, 54)),
        ((), 0, (45, 37, 41, 10, 33)),
        ((3,), 0, (15,)),
        ((13,), 1, (55, 41, 1, 37, 5)),
        ((3,), 1, (15, 33, 1, 13)),
        ((), 1, (37, 1, 41, 33)),
    ),
    (
        ((11,), 0, (46, 34, 19)),
        ((3,), 0, (15, 14)),
        ((), 1, (58, 10, 37)),
        ((15,), 0, (1, 11, 63)),
        ((), 1, (37, 1, 5)),
        ((3,), 0, (33, 15)),
        ((), 0, (5, 14, 41)),
        ((), 0, (5, 9, 45)),
    ),
    (
        ((), 1, (33, 9, 23, 5, 45)),
        ((6,), 1, (33, 41, 9, 25, 1)),
        ((), 0, (33, 45, 1)),
        ((3,), 0, (14, 15, 53, 62, 57)),
        ((4,), 0, (9, 41, 17, 45)),
        ((), 0, (54,)),
        ((13,), 0, (55,)),
        ((5, 3, 13), 0, (23, 15, 54)),
    ),
    (
        ((), 0, (13,)),
        ((), 0, (37, 27, 5, 21, 17)),
        ((15,), 0, (5, 41, 63)),
        ((), 1, (32, 49, 40, 0)),
        ((13,), 0, (14, 18, 55, 13)),
        ((), 0, (14, 13)),
        ((), 0, (45, 37, 9)),
        ((), 1, (13, 14, 4, 44, 43)),
    ),
    (
        ((6,), 0, (1, 47, 27, 26, 41)),
        ((7,), 0, (45, 31, 13)),
        ((3,), 1, (4, 42, 15, 57)),
        ((4,), 0, (36, 16)),
        ((), 0, (53, 49)),
        ((4,), 1, (16, 8, 19, 4, 17)),
        ((6,), 1, (8, 25, 32)),
        ((), 0, (49,)),
    ),
    (
        ((7,), 1, (0, 37, 30)),
        ((12,), 1, (4, 50)),
        ((5,), 0, (13, 36, 23)),
        ((), 0, (13, 44, 4, 18)),
        ((), 1, (44, 36, 19, 33, 32)),
        ((), 0, (9, 45, 49)),
        ((), 0, (4, 54)),
        ((), 0, (55, 40, 21)),
    ),
    (
        ((), 0, (21, 32, 31)),
        ((), 0, (0, 40, 20)),
        ((), 0, (9, 0, 21)),
        ((), 0, (61, 12, 48, 8)),
        ((), 0, (8, 12)),
        ((6,), 0, (27, 0, 40)),
        ((4,), 0, (18, 44, 53, 12, 19)),
        ((14,), 0, (57, 22, 32, 0)),
    ),
    (
        ((), 0, (44, 8, 4)),
        ((13,), 0, (24, 54, 36)),
        ((4,), 0, (17, 53, 8, 14)),
        ((6, 5), 0, (25, 52, 20)),
        ((6, 5), 0, (24, 16, 4, 23)),
        ((15, 5), 0, (63, 21)),
        ((5, 14), 0, (23, 59, 0, 22)),
        ((15, 7), 0, (8, 61, 30, 58)),
    ),
    (
        ((12,), 0, (51,)),
        ((), 0, (26, 49)),
        ((6,), 0, (20, 26, 12, 52)),
        ((), 0, (24, 27, 56)),
        ((14, 15), 0, (57, 61, 25, 21, 0)),
        ((14,), 0, (61, 32, 59)),
        ((15, 7), 0, (57, 61, 30, 17, 58)),
        ((), 0, (62,)),
    ),
    (
        ((13,), 0, (50, 55, 17, 49)),
        ((), 0, (30, 12, 8, 55)),
        ((), 0, (22, 16, 25, 49, 24)),
        ((), 0, (19,)),
        ((7,), 0, (20, 62, 58, 48, 28)),
        ((), 0, (36, 62, 23)),
        ((), 0, (31, 56, 29, 49)),
        ((6,), 0, (31, 29, 59, 24, 20)),
    ),
    (
        ((14,), 0, (12, 59, 54)),
        ((), 0, (16, 32, 53, 44)),
        ((), 0, (32, 62, 19)),
        ((), 0, (26,)),
        ((), 0, (54,)),
        ((7,), 0, (12, 30, 57)),
        ((), 0, (20, 62, 16, 27)),
        ((4,), 0, (17, 12, 25, 52)),
    ),
    (
        ((), 0, (36, 53, 57)),
        ((15, 14), 0, (28, 62, 59, 57, 51)),
        ((7,), 0, (61, 18, 40, 28)),
        ((7,), 0, (28, 29, 17)),
        ((), 0, (59, 56, 30)),
        ((), 0, (18, 48, 58, 52, 24)),
        ((), 0, (48, 26, 40)),
        ((), 0, (16, 28)),
    ),
    (
        ((15,), 0, (40, 20, 24, 25, 63)),
        ((), 0, (58, 48, 56, 63, 52)),
        ((), 0, (31, 48)),
        ((), 0, (22,)),
        ((), 0, (27, 52, 26)),
        ((), 0, (56, 31, 20, 44)),
        ((), 0, (52, 21, 36)),
        ((), 0, (36, 18, 53)),
    ),
    (
        ((), 0, (29, 48, 61, 58, 62)),
        ((), 0, (29,)),
        ((), 0, (44, 27)),
        ((), 0, (21,)),
        ((), 0, (22,)),
        ((), 0, (28, 53, 26, 60, 25)),
        ((), 0, ()),
        ((), 0, (26, 27, 63)),
    ),
    (
        ((), 0, (28, 52, 16, 56, 60)),
        ((), 0, (61, 60)),
        ((), 0, (29, 60, 30, 56)),
        ((), 0, (23, 30, 60, 31)),
        ((), 0, (40, 63, 29, 60, 31)),
        ((), 0, (22, 29)),
        ((), 0, (63, 60, 28, 24)),
        ((), 0, (48, 56, 60, 19)),
    ),
)


def quarter(dy, i):
    odd = dy % 2
    return (1 - odd) * (2 * (i % 2) + i // 2) + odd * ((i + 3 - dy) % 4)


def kernel(
    feats, starts, sw, taps, bias, w_ref, out_ref,
    rtaps, passing, fbuf, ext, gbuf, toep, xs, conv, mix, wts, part, got1, got2, done,
    f_sem, halo_ss, halo_rs, pass_rs, pass_ss, zx_ss, w_rs, sib_ss, zp_ss, zm_ss, x_ss, mix_ss, mix_rs,
    p_ss, got1_rs, got2_rs, out_sem,
):
    c, t = lax.axis_index("ctx"), lax.axis_index("tp")
    xh, z, k = c // 8, (c // 2) % 4, c % 2
    y, xl = t // 2, t % 2
    role = (xl + z) % 2

    def dev(xh, z, k, y, xl):
        return ((xh * 4 + z) * 2 + k, y * 2 + xl)

    sib = dev(xh, z, 1 - k, y, xl)
    zp, zm = dev(xh, (z + 1) % 4, k, y, xl), dev(xh, (z + 3) % 4, k, y, xl)
    yp, ym = dev(xh, z, k, (y + 1) % 4, xl), dev(xh, z, k, (y + 3) % 4, xl)
    xp, xn = dev(xh, z, k, y, 1 - xl), dev(1 - xh, z, k, y, 1 - xl)
    nxt, prv = ((c + 1) % 16, t), ((c + 15) % 16, t)

    f_copies = []
    for s in range(3):
        cp = pltpu.make_async_copy(feats.at[s], fbuf.at[s, pl.ds(HALO, ROWS)], f_sem.at[s])
        cp.start()
        f_copies.append(cp)

    barrier = pltpu.get_barrier_semaphore()
    for d in (sib, zp, zm, yp, ym, xp, xn, prv):
        pl.semaphore_signal(barrier, inc=1, device_id=d, device_id_type=MESH)
    pl.semaphore_wait(barrier, 8)

    def remote(src, dst, ss, rs, d):
        return pltpu.make_async_remote_copy(
            src_ref=src, dst_ref=dst, send_sem=ss, recv_sem=rs, device_id=d, device_id_type=MESH
        )

    dy_own = (2 * xh + z // 2 - y + 4) % 4

    def w_piece(h):
        return w_ref.at[:, pl.ds(h * LANES, LANES)]

    def slot(dy, h, r, core):
        return wts.at[dy, h, r, :, pl.ds(pl.multiple_of(core * LANES, LANES), LANES)]

    def x_copy(i, side):
        h = quarter(dy_own, i)
        return remote(
            w_piece(h), slot(dy_own, h, 1, k), x_ss.at[i, side], w_rs.at[dy_own, h, 1, k], (xp, xn)[side]
        )

    def pass_copy(i):
        h = quarter(dy_own, i)
        return remote(w_piece(h), passing.at[i], x_ss.at[i, 0], pass_rs.at[i], xp)

    def z_pass_copy(i, side):
        h = quarter(dy_own, i)
        return remote(
            w_piece(h), passing.at[4 * side + i], zx_ss.at[i, side], pass_rs.at[4 * side + i], (zp, zm)[side]
        )

    def z_onward_copy(i, side):
        dy = (2 * xh + ((z + 3 + 2 * side) % 4) // 2 - y + 4) % 4
        h = quarter(dy, i)
        return remote(
            passing.at[4 * side + i], slot(dy, h, 1, k), pass_ss.at[4 * side + i], w_rs.at[dy, h, 1, k], xn
        )

    def onward_copy(i):
        h = quarter(dy_own, i)
        return remote(passing.at[i], slot(dy_own, h, 0, k), pass_ss.at[i], w_rs.at[dy_own, h, 0, k], xn)

    halo_f = remote(
        feats.at[:, pl.ds(ROWS - HALO, HALO)], fbuf.at[:, pl.ds(0, HALO)], halo_ss.at[0], halo_rs.at[0], nxt
    )
    halo_f.start()

    @pl.when(role == 0)
    def _():
        for i in range(4):
            h = quarter(dy_own, i)
            pltpu.make_async_copy(w_piece(h), slot(dy_own, h, 0, k), w_rs.at[dy_own, h, 0, k]).start()

    def sib_copy(dy, h, r):
        here = slot(dy, h, r, k)
        return remote(here, here, sib_ss.at[dy, h, r], w_rs.at[dy, h, r, k], sib)

    def zp_copy(dy, h, r):
        here = slot(dy, h, r, k)
        return remote(here, here, zp_ss.at[dy, h, r], w_rs.at[dy, h, r, k], zp)

    def zm_copy(dy, h, r):
        here = slot(dy, h, r, k)
        return remote(here, here, zm_ss.at[dy, h, r], w_rs.at[dy, h, r, k], zm)

    def w_wait(dy, h, r, core):
        here = slot(dy, h, r, core)
        remote(here, here, sib_ss.at[dy, h, r], w_rs.at[dy, h, r, core], sib).wait_recv()

    kind_here = (z // 2 + y) % 2
    kind_below = (((z + 3) % 4) // 2 + y) % 2
    first_odd = 1 + 2 * ((((y + 1) % 4) // 2 + xh) % 2)

    def unit_of(kind, u):
        dy0, i0 = 2 - 2 * (u // 4), u % 4
        odd = u % 2
        dy1, i1 = first_odd * (1 - odd) + (4 - first_odd) * odd, u // 2
        dy, i = dy0 + kind * (dy1 - dy0), i0 + kind * (i1 - i0)
        return dy, quarter(dy, i)

    def side_of(dy):
        return (((y + dy) % 4) // 2 + xh) % 2

    def piece_of(kind, n):
        dy, h = unit_of(kind, n // 2)
        return dy, h, (n + side_of(dy)) % 2

    far_side = side_of(2)
    kind = kind_here + role * (kind_below - kind_here)
    cls = role * 4 + kind * 2 + far_side

    def pick(values):
        a, b, c2, d = values
        if a == b == c2 == d:
            return a
        return a + far_side * (b - a) + kind * (c2 - a) + kind * far_side * (d - c2 - b + a)

    def pick_any(values):
        if all(v == values[0] for v in values):
            return values[0]
        picked = jnp.int32(values[0])
        for n in range(1, 8):
            picked = jnp.where(cls == n, jnp.int32(values[n]), picked)
        return picked

    def xp_step(n):
        @pl.when(role == 0)
        def _():
            pass_copy(n).start()

        @pl.when(role == 1)
        def _():
            x_copy(n, 0).start()

    def z_pass_step(n):
        z_pass_copy(n, 0).start()
        z_pass_copy(n, 1).start()

    def z_onward_step(n):
        for side in range(2):
            z_pass_copy(n, side).wait_recv()
            z_onward_copy(n, side).start()

    def at(which, base, n):
        code = jnp.int32(0)
        for m in range(16):
            code = jnp.where(n == m, pick([ORDERS[base + q][which][m] for q in range(4)]), code)
        return code

    def spread_step(n):
        code = at(0, 0, n)
        t, i = code // 4, code % 4
        dy = (dy_own + 2 * (t // 2)) % 4
        h, r = quarter(dy, i), t % 2
        w_wait(dy, h, r, k)

        @pl.when(t != 3)
        def _():
            zp_copy(dy, h, r).start()
            zm_copy(dy, h, r).start()

        sib_copy(dy, h, r).start()

    def relay_step(n):
        dy, h, r = piece_of(1 - kind_here, at(1, 0, n))
        w_wait(dy, h, r, k)
        sib_copy(dy, h, r).start()

    def xn_step(n):
        i = n // 2

        @pl.when(n % 2 == 0)
        def _():
            x_copy(i, 1).start()

        @pl.when(n % 2 == 1)
        def _():
            pass_copy(i).wait_recv()
            onward_copy(i).start()

    def from_below_step(n):
        dy, h, r = piece_of(kind_below, at(0, 4, n))
        w_wait(dy, h, r, k)

        @pl.when(r == 0)
        def _():
            zp_copy(dy, h, r).start()

        sib_copy(dy, h, r).start()

    def from_above_step(n):
        dy, h, r = piece_of(1 - kind_below, at(1, 4, n))
        w_wait(dy, h, r, k)

        @pl.when(r == 1)
        def _():
            zm_copy(dy, h, r).start()

        sib_copy(dy, h, r).start()

    sequences = (
        (xp_step, z_onward_step, spread_step, relay_step),
        (xp_step, z_pass_step, xn_step, from_below_step, from_above_step),
    )

    def transfers(point):
        for r in range(2):
            now = TRANSFERS[point][4 * r : 4 * r + 4]
            then = TRANSFERS[point - 1][4 * r : 4 * r + 4] if point else ((0,) * 5,) * 4
            if now == then:
                continue

            @pl.when(role == r)
            def _():
                for q, step in enumerate(sequences[r]):
                    lo, hi = [v[q] for v in then], [v[q] for v in now]
                    if lo != hi:
                        def body(n, _, step=step):
                            step(n)
                            return 0

                        lax.fori_loop(pick(lo), pick(hi), body, 0)

    ends = lax.broadcasted_iota(jnp.int32, (BLK, BLK), 0) + lax.broadcasted_iota(jnp.int32, (BLK, BLK), 1)
    mirror = (ends == BLK - 1).astype(F32).astype(BF16)
    rtaps[:, pl.ds(0, BLK)] = jnp.dot(taps[...].astype(BF16), mirror, preferred_element_type=F32)
    rtaps[:, pl.ds(BLK, BLK)] = jnp.zeros((CH // GROUP, BLK), F32)

    def toep_body(g, _):
        row = jnp.broadcast_to(rtaps[pl.ds(g, 1)], (BLK, 2 * BLK))
        toep[g] = pltpu.roll(row, 1, 1, stride=1, stride_axis=0).astype(BF16)
        return 0

    transfers(0)
    lax.fori_loop(0, CH // GROUP // 2, toep_body, 0)
    transfers(1)
    lax.fori_loop(CH // GROUP // 2, CH // GROUP, toep_body, 0)
    transfers(2)

    first = (c > 0).astype(F32)

    def keep_of(b):
        kept = (1 - starts[b]).astype(F32)
        return kept * jnp.where(b == 0, first, 1.0)

    def short(s, b, keep, lanes):
        tail = fbuf[s, pl.ds(pl.multiple_of(b * BLK, BLK), HALO), lanes].astype(F32)
        ext[s, pl.ds(0, 8), lanes] = tail[8:] * keep
        ext[s, pl.ds(8, BLK), lanes] = fbuf[
            s, pl.ds(pl.multiple_of(b * BLK + HALO, HALO), BLK), lanes
        ].astype(F32)
        total = sw[s, pl.ds(0, 1), lanes] * ext[s, pl.ds(8, BLK), lanes]
        for j in range(1, SPAN):
            total += sw[s, pl.ds(j, 1), lanes] * ext[s, pl.ds(8 - j, BLK), lanes]
        return total

    def lanes_of(lt):
        return pl.ds(pl.multiple_of(lt * LANES, LANES), LANES)

    def gate(b):
        keep = keep_of(b)

        def body(lt, _):
            lanes = lanes_of(lt)
            gbuf[b + 1, :, lanes] = (short(1, b, keep, lanes) * short(2, b, keep, lanes)).astype(BF16)
            return 0

        lax.fori_loop(0, CH // LANES, body, 0)

    def mix_copy(m):
        rows = pl.ds(m * CHUNK, CHUNK)
        return remote(mix.at[0, rows], mix.at[1, rows], mix_ss.at[m], mix_rs.at[m], xp)

    lane_group = lax.broadcasted_iota(jnp.int32, (BLK, 2 * LANES), 1) % LANES // GROUP

    def mix_pair(b0, lo, hi):
        keeps = [keep_of(b0), keep_of(b0 + 1)]

        def body(lt, _):
            lanes = lanes_of(lt)
            for i in range(2):
                cols = pl.ds(i * LANES, LANES)
                xs[pl.ds(0, BLK), cols] = (gbuf[b0 + i, :, lanes].astype(F32) * keeps[i]).astype(BF16)
                xs[pl.ds(BLK, BLK), cols] = gbuf[b0 + i + 1, :, lanes]
            mats = toep[pl.ds(lt * PER_TILE, PER_TILE)].reshape(PER_TILE * BLK, 2 * BLK)
            every = jnp.dot(mats, xs[...], preferred_element_type=F32)
            every = every.reshape(PER_TILE, BLK, 2 * LANES)
            picked = every[0]
            for g in range(1, PER_TILE):
                picked = jnp.where(lane_group == g, every[g], picked)
            conv[...] = picked
            for i in range(2):
                gated = gbuf[b0 + i + 1, :, lanes].astype(F32)
                query = short(0, b0 + i, keeps[i], lanes)
                direct = conv[:, pl.ds(i * LANES, LANES)] + bias[:, lanes] * gated
                mix[0, pl.ds(pl.multiple_of((b0 + i) * BLK, BLK), BLK), lanes] = (query * direct).astype(BF16)
            return 0

        lax.fori_loop(lo, hi, body, 0)

    chunk_at = [NCHUNK - 1 - i for i in range(NCHUNK)]

    tiles = CH // LANES
    for cp in f_copies:
        cp.wait()
    gate(NB - 1)
    halo_g = remote(gbuf.at[NB], gbuf.at[0], halo_ss.at[1], halo_rs.at[1], nxt)
    halo_g.start()
    transfers(3)
    point = 4
    for m in chunk_at:
        if m > 0:
            gate(2 * m)
            gate(2 * m - 1)
        else:
            halo_f.wait_recv()
            gate(0)
            halo_g.wait_recv()
        transfers(point)
        point += 1
        if m == NCHUNK - 1:
            mix_pair(2 * m, 0, tiles // 2)
            transfers(point)
            point += 1
            mix_pair(2 * m, tiles // 2, tiles)
        else:
            mix_pair(2 * m, 0, tiles)
        mix_copy(m).start()
        transfers(point)
        point += 1

    def rows_of(m):
        return pl.ds(pl.multiple_of(m * CHUNK, CHUNK), CHUNK)

    def project(dy, h, m):
        rows = rows_of(m)
        total = jnp.dot(mix[0, rows], wts[dy, h, 0], preferred_element_type=F32)
        return total + jnp.dot(mix[1, rows], wts[dy, h, 1], preferred_element_type=F32)

    def to_y(dy):
        return dev(xh, z, k, (y + dy) % 4, xl)

    def far_copy(v, m):
        dy, h = 2, quarter(2, v)
        here = part.at[dy, h, rows_of(m)]
        return remote(here, got1.at[h, rows_of(m)], p_ss.at[dy, h, m], got1_rs.at[h, m], to_y(1 + 2 * (v % 2)))

    def near_copy(u, m):
        dy, h = unit_of(1, u)
        here = part.at[dy, h, rows_of(m)]
        there = got2.at[dy // 2, h, rows_of(m)]
        return remote(here, there, p_ss.at[dy, h, m], got2_rs.at[dy // 2, h, m], to_y(dy))

    def got1_wait(h, m):
        there = got1.at[h, rows_of(m)]
        remote(there, there, p_ss.at[0, h, m], got1_rs.at[h, m], yp).wait_recv()

    def got2_wait(side, h, m):
        there = got2.at[side, h, rows_of(m)]
        remote(there, there, p_ss.at[0, h, m], got2_rs.at[side, h, m], yp).wait_recv()

    def tile_step(_, packed):
        code = packed % 64
        knd, u, m = code // 32, code // 4 % 8, code % 4
        dy, h = unit_of(knd, u)
        rows = rows_of(m)
        total = project(dy, h, m)
        depends = (knd == 1) & (u >= 4)

        @pl.when(depends)
        def _():
            got1_wait(h, m)
            part[dy, h, rows] = (total + got1[h, rows].astype(F32)).astype(BF16)

        @pl.when(jnp.logical_not(depends))
        def _():
            part[dy, h, rows] = total.astype(BF16)

        @pl.when((knd == 0) & (u < 4))
        def _():
            far_copy(u, m).start()

        @pl.when(knd == 1)
        def _():
            near_copy(u, m).start()

        return packed // 64

    chunks = [0] * 8
    for p, phase in enumerate(PHASES):
        if p:
            transfers(point)
            point += 1
        for n, (waits, _, _) in enumerate(phase):
            if waits:
                @pl.when(cls == n)
                def _():
                    for code in waits:
                        dy, h = unit_of(code // 8, code % 8)
                        for r in range(2):
                            w_wait(dy, h, r, 1 - k)

        before = list(chunks)
        chunks = [a + row[1] for a, row in zip(chunks, phase)]
        if before != chunks:
            def chunk_step(n, _):
                mix_copy(NCHUNK - 1 - n).wait_recv()
                return 0

            lax.fori_loop(pick_any(before), pick_any(chunks), chunk_step, 0)
        packed = [sum(code * 64**n for n, code in enumerate(row[2])) for row in phase]
        lax.fori_loop(0, pick_any([len(row[2]) for row in phase]), tile_step, pick_any(packed) + jnp.int32(0))

    halo_f.wait_send()
    halo_g.wait_send()
    for m in range(NCHUNK):
        mix_copy(m).wait_send()

    def sent_body(u, _):
        for knd in range(2):
            dy, h = unit_of(knd, u)
            for r in range(2):
                sib_copy(dy, h, r).wait_send()

        @pl.when(role == 1)
        def _():
            dya, ha = unit_of(kind_below, u)
            dyb, hb = unit_of(1 - kind_below, u)
            zp_copy(dya, ha, 0).wait_send()
            zm_copy(dyb, hb, 1).wait_send()

        return 0

    lax.fori_loop(0, 8, sent_body, 0)

    def early_sent_body(v, _):
        for m in range(NCHUNK):
            far_copy(v, m).wait_send()
            near_copy(v, m).wait_send()

        @pl.when(role == 0)
        def _():
            pass_copy(v).wait_send()
            for t in range(3):
                dy = (dy_own + 2 * (t // 2)) % 4
                zp_copy(dy, quarter(dy, v), t % 2).wait_send()
                zm_copy(dy, quarter(dy, v), t % 2).wait_send()
            z_onward_copy(v, 0).wait_send()
            z_onward_copy(v, 1).wait_send()

        @pl.when(role == 1)
        def _():
            x_copy(v, 0).wait_send()
            x_copy(v, 1).wait_send()
            onward_copy(v).wait_send()
            z_pass_copy(v, 0).wait_send()
            z_pass_copy(v, 1).wait_send()

        return 0

    lax.fori_loop(0, 4, early_sent_body, 0)

    def out_copy(h, m):
        rows = rows_of(m)
        for core in range(2):
            yield pltpu.make_async_copy(
                done.at[h, rows, pl.ds(core * LANES, LANES)],
                out_ref.at[rows, pl.ds(pl.multiple_of(core * 512 + h * LANES, LANES), LANES)],
                out_sem.at[h, m, core],
            )

    def sum_body(n, _):
        i, m = n // NCHUNK, NCHUNK - 1 - n % NCHUNK
        h = 2 * (i % 2) + i // 2
        rows = rows_of(m)
        got2_wait(0, h, m)
        got2_wait(1, h, m)
        total = part[0, h, rows].astype(F32) + got2[0, h, rows].astype(F32) + got2[1, h, rows].astype(F32)
        done[h, rows] = total.astype(done.dtype)
        for cp in out_copy(h, m):
            cp.start()
        return 0

    def late_sent_body(u, _):
        for m in range(NCHUNK):
            near_copy(u, m).wait_send()
        return 0

    def out_body(h, _):
        for m in range(NCHUNK):
            for cp in out_copy(h, m):
                cp.wait()
        return 0

    lax.fori_loop(0, 3 * NCHUNK, sum_body, 0)
    lax.fori_loop(0, 3, out_body, 0)
    lax.fori_loop(4, 6, late_sent_body, 0)
    lax.fori_loop(3 * NCHUNK, 4 * NCHUNK, sum_body, 0)
    lax.fori_loop(6, 8, late_sent_body, 0)
    out_body(3, 0)


def on_device(features, contig_starts, short_filter, medium_filter, filter_bias, out_weight):
    vmem = pl.BlockSpec(memory_space=pltpu.VMEM)
    hbm = pl.BlockSpec(memory_space=pl.ANY)
    dma = pltpu.SemaphoreType.DMA
    return pl.pallas_call(
        kernel,
        out_shape=jax.ShapeDtypeStruct((ROWS, CH), OUT),
        in_specs=[hbm, pl.BlockSpec(memory_space=pltpu.SMEM), vmem, vmem, vmem, hbm],
        out_specs=hbm,
        scratch_shapes=[
            pltpu.VMEM((CH // GROUP, 2 * BLK), F32),
            pltpu.VMEM((8, CH, LANES), BF16),
            pltpu.VMEM((3, HALO + ROWS, CH), BF16),
            pltpu.VMEM((3, 8 + BLK, CH), F32),
            pltpu.VMEM((NB + 1, BLK, CH), BF16),
            pltpu.VMEM((CH // GROUP, BLK, 2 * BLK), BF16),
            pltpu.VMEM((2 * BLK, 2 * LANES), BF16),
            pltpu.VMEM((BLK, 2 * LANES), F32),
            pltpu.VMEM((2, ROWS, CH), BF16),
            pltpu.VMEM((4, 4, 2, CH, 2 * LANES), BF16),
            pltpu.VMEM((4, 4, ROWS, 2 * LANES), BF16),
            pltpu.VMEM((4, ROWS, 2 * LANES), BF16),
            pltpu.VMEM((2, 4, ROWS, 2 * LANES), BF16),
            pltpu.VMEM((4, ROWS, 2 * LANES), OUT),
            dma((3,)),
            dma((2,)),
            dma((2,)),
            dma((8,)),
            dma((8,)),
            dma((4, 2)),
            dma((4, 4, 2, 2)),
            dma((4, 4, 2)),
            dma((4, 4, 2)),
            dma((4, 4, 2)),
            dma((4, 2)),
            dma((NCHUNK,)),
            dma((NCHUNK,)),
            dma((4, 4, NCHUNK)),
            dma((4, NCHUNK)),
            dma((2, 4, NCHUNK)),
            dma((4, NCHUNK, 2)),
        ],
        compiler_params=pltpu.CompilerParams(
            collective_id=0, has_side_effects=True, vmem_limit_bytes=60 * 1024 * 1024
        ),
        cost_estimate=pl.CostEstimate(
            flops=2 * ROWS * 2048 * 4096, bytes_accessed=16 * 1024 * 1024, transcendentals=0
        ),
    )(
        jnp.transpose(features, (1, 0, 2)),
        contig_starts,
        jnp.transpose(short_filter, (1, 0, 2)),
        medium_filter,
        filter_bias.reshape(1, CH),
        out_weight,
    )


def solution(mesh):
    in_specs = (
        P("ctx", None, "tp"),
        P("ctx"),
        P(None, None, "tp"),
        P("tp", None),
        P("tp"),
        P("tp", "ctx"),
    )
    out_specs = P("ctx", "tp")
    return jax.shard_map(
        on_device, mesh=mesh, in_specs=in_specs, out_specs=out_specs, check_vma=False
    )
```
